32 devices in a mesh: dp: 2 (over y), blk: 4 (over z), uly: 4 (over x, core).
Axes of the slice: x: 2, y: 2, z: 4, core: 2. Of those that a mesh axis runs over, the one named last changes fastest.
Arguments:
- hidden_states: bfloat16 [2, 4096, 4096], P('dp', ('blk', 'uly')), may hold values from -96 to 96
- block_table: int32 [2, 8, 8], P('dp'), may hold values from 0 to 1, as said below
- w_query: bfloat16 [4096, 2048], P(('dp', 'blk'), 'uly'), may hold values from -0.09375 to 0.09375
- w_key: bfloat16 [4096, 512], P(('dp', 'blk'), 'uly'), may hold values from -0.09375 to 0.09375
- w_value: bfloat16 [4096, 512], P(('dp', 'blk'), 'uly'), may hold values from -0.09375 to 0.09375
Outputs:
- attended: bfloat16 [2, 4096, 2048], P('dp', ('blk', 'uly'))
The draws below stay inside these ranges and needn't reach their ends.
Inputs may be any that keep to these rules, and one draw needn't show every extreme that they name: block_table[s, i, j] is 1 where query block i of sequence s may read key block j, else 0; it is 1 on the diagonal and 0 above it; below the diagonal a block is allowed when it lies within a window of 1 to 4 blocks ending at i, or is one of the sequence's global key blocks; the global key blocks are block 0 and exactly 2 others.
All inputs are finite; a program needn't handle non-finite values.
Results may differ from the reference program's by a relative error of at most 0.024.
The reference program's roundings to bfloat16 on the way count: a program that leaves them out, or rounds other values in their place, can miss the bound.
Values may be sent and summed in bfloat16 or wider, within the bound.
A program may use at most 128 MiB of HBM per device.

```python
import jax
import jax.numpy as jnp
from jax import lax

D = 4096
H = 16
KV = 4
HD = 128
MBLK = 512
WIN = 4
SEQ = 4096
BATCH = 2
NBM = 8


def draw_hidden_states(key, part):
    base_key = jax.random.fold_in(jax.random.fold_in(key, 11), 0)
    values = jax.random.normal(base_key, (BATCH, SEQ, D), jnp.float32)
    return jnp.clip(values, -96.0, 96.0).astype(jnp.bfloat16)


def draw_block_table(key, part):
    global_key, window_key = jax.random.split(jax.random.fold_in(key, 23))
    block_count = NBM
    glob_count = min(8, block_count // 4)
    seq_keys = jax.random.split(global_key, BATCH)
    perms = jax.vmap(lambda one_key: jax.random.permutation(one_key, block_count - 1))(seq_keys) + 1
    chosen = perms[:, :glob_count]
    col_ids = jnp.arange(block_count)
    global_cols = jnp.any(col_ids[None, None, :] == chosen[:, :, None], axis=1) | (col_ids == 0)[None, :]
    global_cols = global_cols[:, None, :]
    window = jax.random.randint(window_key, (BATCH, block_count, 1), 1, WIN + 1)
    row_ids = jnp.arange(block_count)[:, None]
    col_grid = col_ids[None, :]
    allowed = (col_grid <= row_ids)[None] & (((row_ids - col_grid)[None] < window) | global_cols)
    return allowed.astype(jnp.int32)


def block_levels(rng, dims, cuts, smallest, largest):
    def one(axis_at, blocks):
        heights = jax.random.uniform(jax.random.fold_in(jax.random.fold_in(rng, 6), axis_at), (blocks,), jnp.float32, smallest / len(cuts), largest / len(cuts))
        return jnp.repeat(jnp.exp(heights), dims[axis_at] // blocks).reshape((-1,) + (1,) * (len(dims) - axis_at - 1))

    gain = one(*cuts[0])
    for cut in cuts[1:]:
        gain = gain * one(*cut)
    return gain


def centred(rng, extent, spread, bound, cuts=(), kind=jnp.bfloat16):
    drawn = jax.random.normal(rng, extent, jnp.float32) * spread
    if len(cuts) > 0:
        drawn = block_levels(rng, extent, cuts, -0.22, 0.18) * drawn
    return jnp.clip(drawn, min=-bound, max=bound).astype(kind)


def setup_inputs(seed: int = 0) -> dict:
    key_of = jax.random.split(jax.random.key(seed), 6)
    hidden_states = draw_hidden_states(jax.random.fold_in(key_of[5], 71), 0)
    block_table = draw_block_table(jax.random.fold_in(key_of[5], 71), 0)
    w_query = centred(key_of[2], (D, H * HD), D ** -0.5, 0.09375, ((0, 8), (1, 4)))
    w_key = centred(key_of[3], (D, KV * HD), D ** -0.5, 0.09375, ((0, 8), (1, 4)))
    w_value = centred(key_of[4], (D, KV * HD), D ** -0.5, 0.09375, ((0, 8), (1, 4)))
    return {"hidden_states": hidden_states, "block_table": block_table, "w_query": w_query, "w_key": w_key, "w_value": w_value}


THETA_BASE = 500000.0


def rotate(values, positions):
    half_dim = values.shape[-1] // 2
    exponent = jnp.arange(half_dim, dtype=jnp.float32) * (2.0 / values.shape[-1])
    frequency = jnp.power(jnp.float32(THETA_BASE), -exponent)
    angles = positions.astype(jnp.float32)[:, None] * frequency[None, :]
    cosine = jnp.cos(angles)[:, None, :]
    sine_part = jnp.sin(angles)[:, None, :]
    first_half = values[..., :half_dim]
    second = values[..., half_dim:]
    return jnp.concatenate([first_half * cosine - second * sine_part, second * cosine + first_half * sine_part], axis=-1)


def one_sequence(hidden, block_mask, w_query, w_key, w_value):
    positions = jnp.arange(SEQ, dtype=jnp.int32)
    query = jnp.dot(hidden, w_query, preferred_element_type=jnp.float32).reshape(SEQ, H, HD)
    key_rows = jnp.dot(hidden, w_key, preferred_element_type=jnp.float32).reshape(SEQ, KV, HD)
    value_rows = jnp.dot(hidden, w_value, preferred_element_type=jnp.float32).reshape(SEQ, KV, HD).astype(jnp.bfloat16)
    query = rotate(query, positions).astype(jnp.bfloat16)
    key_rows = rotate(key_rows, positions).astype(jnp.bfloat16)
    key_heads = jnp.repeat(key_rows, H // KV, axis=1).astype(jnp.float32)
    value_heads = jnp.repeat(value_rows, H // KV, axis=1).astype(jnp.float32)
    key_block = positions // MBLK
    score_scale = HD ** -0.5

    def tile(offset):
        query_tile = lax.dynamic_slice_in_dim(query, offset, MBLK, 0).astype(jnp.float32)
        row_pos = offset + jnp.arange(MBLK, dtype=jnp.int32)
        scores = jnp.einsum("qhd,khd->hqk", query_tile, key_heads) * score_scale
        allowed = (block_mask[row_pos // MBLK][:, key_block] > 0) & (positions[None, :] <= row_pos[:, None])
        scores = jnp.where(allowed[None], scores, -1e30)
        row_best = jnp.max(scores, axis=2, keepdims=True)
        weights = jnp.exp(scores - row_best)
        row_total = jnp.sum(weights, axis=2)
        rounded = weights.astype(jnp.bfloat16).astype(jnp.float32)
        mixed = jnp.einsum("hqk,khd->qhd", rounded, value_heads)
        return (mixed / row_total.T[:, :, None]).astype(jnp.bfloat16)

    offsets = jnp.arange(SEQ // MBLK, dtype=jnp.int32) * MBLK
    output = lax.map(tile, offsets)
    return output.reshape(SEQ, H * HD)


def reference(hidden_states, block_table, w_query, w_key, w_value):
    results = []
    for sequence in range(BATCH):
        results.append(one_sequence(hidden_states[sequence], block_table[sequence], w_query, w_key, w_value))
    return jnp.stack(results)
```

```python
import functools

import jax
import jax.numpy as jnp
from jax import lax
from jax.experimental import pallas as pl
from jax.experimental.pallas import tpu as pltpu
from jax.sharding import PartitionSpec as P

H = 16
KV = 4
HD = 128
MBLK = 512
THETA_BASE = 500000.0
LOG2E = 1.4426950408889634
NT = (((1,), (1,)), ((), ()))
TN = (((0,), (0,)), ((), ()))


def from_partner(array, axis, distance):
    return lax.ppermute(array, axis, [(i, i ^ 1 << distance) for i in range(lax.axis_size(axis))])


def angle_tables(positions):
    half_dim = HD // 2
    exponent = jnp.arange(half_dim, dtype=jnp.float32) * (2.0 / HD)
    frequency = jnp.power(jnp.float32(THETA_BASE), -exponent)
    angles = positions.astype(jnp.float32)[:, None] * frequency[None, :]
    return jnp.cos(angles), jnp.sin(angles)


def rotate(values, cosine, sine):
    cosine, sine = cosine[:, None, :], sine[:, None, :]
    half_dim = HD // 2
    first, second = values[..., :half_dim], values[..., half_dim:]
    return jnp.concatenate([first * cosine - second * sine, second * cosine + first * sine], axis=-1)


def attend_kernel(heads, tiles, table, rank, q_ref, kv_ref, out_ref, best, total, accum):
    scale = HD**-0.5 * LOG2E

    def visit(q_start, key_block, diagonal):
        k_start = pl.multiple_of(key_block * MBLK, MBLK)
        key = kv_ref[pl.ds(k_start, MBLK), :HD]
        value = kv_ref[pl.ds(k_start, MBLK), HD:]
        for head in range(heads):
            cols = pl.ds(head * MBLK, MBLK)
            query = q_ref[pl.ds(q_start, MBLK), head * HD : (head + 1) * HD]
            scores = lax.dot_general(key, query, NT, preferred_element_type=jnp.float32) * scale
            if diagonal:
                key_at = lax.broadcasted_iota(jnp.int32, (MBLK, MBLK), 0)
                query_at = lax.broadcasted_iota(jnp.int32, (MBLK, MBLK), 1)
                scores = jnp.where(key_at <= query_at, scores, -1e30)
                new_best = jnp.max(scores, axis=0, keepdims=True)
            else:
                old_best = best[:, cols]
                new_best = jnp.maximum(old_best, jnp.max(scores, axis=0, keepdims=True))
            weights = jnp.exp2(scores - new_best)
            sums = jnp.sum(weights, axis=0, keepdims=True)
            mixed = lax.dot_general(
                value, weights.astype(jnp.bfloat16), TN, preferred_element_type=jnp.float32
            )
            best[:, cols] = new_best
            if diagonal:
                total[:, cols] = sums
                accum[:, cols] = mixed
            else:
                rescale = jnp.exp2(old_best - new_best)
                total[:, cols] = total[:, cols] * rescale + sums
                accum[:, cols] = accum[:, cols] * rescale + mixed

    for tile in range(tiles):
        q_start = tile * MBLK
        block = rank[0] * tiles + tile
        visit(q_start, block, True)

        @pl.loop(0, block)
        def _(key_block, q_start=q_start, block=block):
            @pl.when(table[block, key_block] > 0)
            def _():
                visit(q_start, key_block, False)

        for head in range(heads):
            cols = pl.ds(head * MBLK, MBLK)
            final = accum[:, cols] / total[:, cols]
            out_ref[pl.ds(q_start, MBLK), head * HD : (head + 1) * HD] = final.T.astype(jnp.bfloat16)


def attend(table, rank, query, key_value, heads, tiles):
    rows = query.shape[0]
    smem = pl.BlockSpec(memory_space=pltpu.SMEM)
    vmem = pl.BlockSpec(memory_space=pltpu.VMEM)
    return pl.pallas_call(
        functools.partial(attend_kernel, heads, tiles),
        out_shape=jax.ShapeDtypeStruct((rows, heads * HD), jnp.bfloat16),
        in_specs=[smem, smem, vmem, vmem],
        out_specs=vmem,
        scratch_shapes=[
            pltpu.VMEM((1, heads * MBLK), jnp.float32),
            pltpu.VMEM((1, heads * MBLK), jnp.float32),
            pltpu.VMEM((HD, heads * MBLK), jnp.float32),
        ],
        compiler_params=pltpu.CompilerParams(vmem_limit_bytes=48 * 1024 * 1024),
        cost_estimate=pl.CostEstimate(flops=8 * 10**9, bytes_accessed=4 * 10**6, transcendentals=16 * 10**6),
    )(table, rank, query, key_value)


def shards(hidden_states, block_table, w_query, w_key, w_value):
    tokens = hidden_states.shape[1]
    uly_size = lax.axis_size("uly")
    uly_rank = lax.axis_index("uly")
    blk_rank = lax.axis_index("blk")
    heads_here = H // uly_size
    repeats = uly_size // KV
    part_cols = HD // repeats
    query_cols = heads_here * HD
    group_rows = tokens * uly_size
    tiles = group_rows // MBLK
    w_joined = jnp.concatenate([w_query, w_key, w_value], axis=1)
    w_rows = lax.all_gather(w_joined, ("dp", "blk"), axis=0, tiled=True)
    projected = jnp.dot(
        lax.all_gather(hidden_states[0], "uly", axis=0, tiled=True),
        w_rows,
        preferred_element_type=jnp.float32,
    )
    positions = blk_rank * group_rows + jnp.arange(group_rows, dtype=jnp.int32)
    cosine, sine = angle_tables(positions)
    query = rotate(projected[:, :query_cols].reshape(group_rows, heads_here, HD), cosine, sine)
    query = query.astype(jnp.bfloat16).reshape(group_rows, query_cols)
    pieces = jnp.stack(
        [projected[:, query_cols : query_cols + part_cols], projected[:, query_cols + part_cols :]]
    )
    part_index = uly_rank % repeats
    for bit_index in range(repeats.bit_length() - 1):
        partner_piece = from_partner(pieces, "uly", bit_index)
        upper_part = part_index >> bit_index & 1 == 1
        pieces = jnp.where(
            upper_part,
            jnp.concatenate([partner_piece, pieces], axis=-1),
            jnp.concatenate([pieces, partner_piece], axis=-1),
        )
    key = rotate(pieces[0][:, None, :], cosine, sine)[:, 0, :].astype(jnp.bfloat16)
    key_value = jnp.concatenate([key, pieces[1].astype(jnp.bfloat16)], axis=1)
    key_value = lax.all_gather(key_value, "blk", axis=0, tiled=True)
    result = attend(
        block_table[0], blk_rank[None].astype(jnp.int32), query, key_value, heads_here, tiles
    )
    merged = lax.all_to_all(result, "uly", split_axis=0, concat_axis=1, tiled=True)
    return merged[None]


def solution(mesh):
    placed = (
        P("dp", ("blk", "uly"), None),
        P("dp", None, None),
        P(("dp", "blk"), "uly"),
        P(("dp", "blk"), "uly"),
        P(("dp", "blk"), "uly"),
    )
    return jax.shard_map(
        shards, mesh=mesh, in_specs=placed, out_specs=P("dp", ("blk", "uly"), None), check_vma=False
    )
```

```python
import functools

import jax
import jax.numpy as jnp
from jax import lax
from jax.experimental import pallas as pl
from jax.experimental.pallas import tpu as pltpu
from jax.sharding import PartitionSpec as P

H = 16
KV = 4
HD = 128
MBLK = 512
THETA_BASE = 500000.0
LOG2E = 1.4426950408889634
NT = (((1,), (1,)), ((), ()))
TN = (((0,), (0,)), ((), ()))


def from_partner(array, axis, distance):
    return lax.ppermute(array, axis, [(i, i ^ 1 << distance) for i in range(lax.axis_size(axis))])


def angle_tables(positions):
    half_dim = HD // 2
    exponent = jnp.arange(half_dim, dtype=jnp.float32) * (2.0 / HD)
    frequency = jnp.power(jnp.float32(THETA_BASE), -exponent)
    angles = positions.astype(jnp.float32)[:, None] * frequency[None, :]
    return jnp.cos(angles), jnp.sin(angles)


def rotate(values, cosine, sine):
    cosine, sine = cosine[:, None, :], sine[:, None, :]
    half_dim = HD // 2
    first, second = values[..., :half_dim], values[..., half_dim:]
    return jnp.concatenate([first * cosine - second * sine, second * cosine + first * sine], axis=-1)


def attend_kernel(heads, tiles, table, rank, q_ref, kv_ref, out_ref, best, total, accum):
    scale = HD**-0.5 * LOG2E

    def visit(q_start, key_block, diagonal):
        k_start = pl.multiple_of(key_block * MBLK, MBLK)
        key = kv_ref[pl.ds(k_start, MBLK), :HD]
        value = kv_ref[pl.ds(k_start, MBLK), HD:]
        for head in range(heads):
            cols = pl.ds(head * MBLK, MBLK)
            query = q_ref[pl.ds(q_start, MBLK), head * HD : (head + 1) * HD]
            scores = lax.dot_general(key, query, NT, preferred_element_type=jnp.float32) * scale
            if diagonal:
                key_at = lax.broadcasted_iota(jnp.int32, (MBLK, MBLK), 0)
                query_at = lax.broadcasted_iota(jnp.int32, (MBLK, MBLK), 1)
                scores = jnp.where(key_at <= query_at, scores, -1e30)
                new_best = jnp.max(scores, axis=0, keepdims=True)
            else:
                old_best = best[:, cols]
                new_best = jnp.maximum(old_best, jnp.max(scores, axis=0, keepdims=True))
            weights = jnp.exp2(scores - new_best)
            sums = jnp.sum(weights, axis=0, keepdims=True)
            mixed = lax.dot_general(
                value, weights.astype(jnp.bfloat16), TN, preferred_element_type=jnp.float32
            )
            best[:, cols] = new_best
            if diagonal:
                total[:, cols] = sums
                accum[:, cols] = mixed
            else:
                rescale = jnp.exp2(old_best - new_best)
                total[:, cols] = total[:, cols] * rescale + sums
                accum[:, cols] = accum[:, cols] * rescale + mixed

    for tile in range(tiles):
        q_start = tile * MBLK
        block = rank[0] * tiles + tile
        visit(q_start, block, True)

        @pl.loop(0, block)
        def _(key_block, q_start=q_start, block=block):
            @pl.when(table[block, key_block] > 0)
            def _():
                visit(q_start, key_block, False)

        for head in range(heads):
            cols = pl.ds(head * MBLK, MBLK)
            final = accum[:, cols] / total[:, cols]
            out_ref[pl.ds(q_start, MBLK), head * HD : (head + 1) * HD] = final.T.astype(jnp.bfloat16)


def attend(table, rank, query, key_value, heads, tiles):
    rows = query.shape[0]
    smem = pl.BlockSpec(memory_space=pltpu.SMEM)
    vmem = pl.BlockSpec(memory_space=pltpu.VMEM)
    return pl.pallas_call(
        functools.partial(attend_kernel, heads, tiles),
        out_shape=jax.ShapeDtypeStruct((rows, heads * HD), jnp.bfloat16),
        in_specs=[smem, smem, vmem, vmem],
        out_specs=vmem,
        scratch_shapes=[
            pltpu.VMEM((1, heads * MBLK), jnp.float32),
            pltpu.VMEM((1, heads * MBLK), jnp.float32),
            pltpu.VMEM((HD, heads * MBLK), jnp.float32),
        ],
        compiler_params=pltpu.CompilerParams(vmem_limit_bytes=48 * 1024 * 1024),
        cost_estimate=pl.CostEstimate(flops=8 * 10**9, bytes_accessed=4 * 10**6, transcendentals=16 * 10**6),
    )(table, rank, query, key_value)


PIECE = 256
MESH = pl.DeviceIdType.MESH
HIDDEN_STEPS = 6


def project_kernel(
    dp_n, blk_n, hid, wq, wk, wv, cos_ref, sin_ref, q_out, kv_out,
    weights, rows_all, acc, kv, local_sem, w_send, w_recv, h_send, h_recv, kv_send, kv_recv,
):
    y, z, u = lax.axis_index("dp"), lax.axis_index("blk"), lax.axis_index("uly")
    last = blk_n - 1
    chunks = dp_n * blk_n
    pieces = weights.shape[0]
    tokens = hid.shape[0]
    depth = wq.shape[0]
    group = rows_all.shape[1]
    up, down, across = {"blk": z + 1}, {"blk": z - 1}, {"dp": 1 - y}
    core = u + 1 - 2 * (u % 2)
    chip = (u + 2) % 4
    far = (core + 2) % 4
    mine = y * blk_n + z

    barrier = pltpu.get_barrier_semaphore()

    @pl.when(z < last)
    def _():
        pl.semaphore_signal(barrier, inc=1, device_id=up, device_id_type=MESH)

    @pl.when(z > 0)
    def _():
        pl.semaphore_signal(barrier, inc=1, device_id=down, device_id_type=MESH)

    for where in (across, {"uly": core}, {"uly": chip}):
        pl.semaphore_signal(barrier, inc=1, device_id=where, device_id_type=MESH)

    own = [
        pltpu.make_async_copy(wk, weights.at[0, mine, :, pl.ds(0, HD)], local_sem.at[0]),
        pltpu.make_async_copy(wv, weights.at[0, mine, :, pl.ds(HD, HD)], local_sem.at[1]),
    ]
    for p in range(1, pieces):
        own.append(
            pltpu.make_async_copy(
                wq.at[:, pl.ds((p - 1) * PIECE, PIECE)], weights.at[p, mine], local_sem.at[p + 1]
            )
        )
    for c in range(chunks):
        own.append(
            pltpu.make_async_copy(
                hid.at[:, pl.ds(c * depth, depth)],
                rows_all.at[c, pl.ds(u * tokens, tokens)],
                local_sem.at[pieces + 1 + c],
            )
        )
    for copy in own:
        copy.start()
    middle = jnp.where((z > 0) & (z < last), 1, 0)
    pl.semaphore_wait(barrier, 4 + middle)

    def weight_copy(p, way, source_z, where, rank):
        return pltpu.make_async_remote_copy(
            src_ref=weights.at[p, rank], dst_ref=weights.at[p, rank],
            send_sem=w_send.at[p, way, source_z], recv_sem=w_recv.at[p, rank],
            device_id=where, device_id_type=MESH,
        )

    def hidden_copy(kind, c, source, where):
        part = rows_all.at[c, pl.ds(source * tokens, tokens)]
        return pltpu.make_async_remote_copy(
            src_ref=part, dst_ref=part, send_sem=h_send.at[kind, c], recv_sem=h_recv.at[kind, c],
            device_id={"uly": where}, device_id_type=MESH,
        )

    def kv_copy(source_z):
        return pltpu.make_async_remote_copy(
            src_ref=kv.at[source_z], dst_ref=kv.at[source_z],
            send_sem=kv_send.at[source_z], recv_sem=kv_recv.at[source_z],
            device_id=up, device_id_type=MESH,
        )

    def own_weights(p, finish=False):
        act = (lambda c: c.wait_send()) if finish else (lambda c: c.start())

        @pl.when(z < last)
        def _():
            act(weight_copy(p, 0, z, up, mine))

        @pl.when(z > 0)
        def _():
            act(weight_copy(p, 1, z, down, mine))

        act(weight_copy(p, 2, z, across, mine))

    def pass_on(p, d, finish=False):
        act = (lambda c: c.wait_send()) if finish else (lambda c: c.start())

        @pl.when(z >= d)
        def _():
            rank = y * blk_n + z - d
            if not finish:
                weight_copy(p, 0, z - d, across, rank).wait_recv()

            @pl.when(z < last)
            def _():
                act(weight_copy(p, 0, z - d, up, rank))

            act(weight_copy(p, 2, z - d, across, rank))

        @pl.when(z + d <= last)
        def _():
            rank = y * blk_n + z + d
            if not finish:
                weight_copy(p, 1, z + d, across, rank).wait_recv()

            @pl.when(z > 0)
            def _():
                act(weight_copy(p, 1, z + d, down, rank))

            act(weight_copy(p, 2, z + d, across, rank))

    def across_arrived(p, d):
        other = (1 - y) * blk_n
        if d == 0:
            weight_copy(p, 2, z, across, other + z).wait_recv()
            return

        @pl.when(z >= d)
        def _():
            weight_copy(p, 2, z - d, across, other + z - d).wait_recv()

        @pl.when(z + d <= last)
        def _():
            weight_copy(p, 2, z + d, across, other + z + d).wait_recv()

    def multiply(ps, c):
        @pl.loop(0, group // PIECE)
        def _(i):
            at = pl.ds(pl.multiple_of(i * PIECE, PIECE), PIECE)
            left = rows_all[c, at, :]
            for p in ps:
                acc[p, at, :] += jnp.dot(left, weights[p, c], preferred_element_type=jnp.float32)

    def hidden_ready(c):
        hidden_copy(0, c, core, core).wait_recv()
        hidden_copy(2, c, far, core).wait_recv()

    def turn(values, at):
        return values * cos_ref[at, :] + pltpu.roll(values, HD // 2, 1) * sin_ref[at, :]

    def query_chunks(d):
        for p in range(1, pieces):
            across_arrived(p, d)
        ps = tuple(range(1, pieces))
        if d == 0:
            multiply(ps, mine)
            multiply(ps, (1 - y) * blk_n + z)
            return

        @pl.when(z >= d)
        def _():
            multiply(ps, y * blk_n + z - d)
            multiply(ps, (1 - y) * blk_n + z - d)

        @pl.when(z + d <= last)
        def _():
            multiply(ps, y * blk_n + z + d)
            multiply(ps, (1 - y) * blk_n + z + d)

    def kv_pass(d):
        @pl.when(z >= d)
        def _():
            kv_copy(z - d).wait_recv()

            @pl.when(z < last)
            def _():
                kv_copy(z - d).start()

    own[0].wait()
    own[1].wait()
    own_weights(0)
    for c in range(chunks):
        own[pieces + 1 + c].wait()
        if c < 3:
            hidden_copy(1, c, u, chip).start()
    for c in range(chunks):
        hidden_copy(0, c, u, core).start()
    for p in range(1, pieces):
        own[p + 1].wait()
    acc[...] = jnp.zeros_like(acc)

    chunk_ends = [-(-chunks * (s + 1) // HIDDEN_STEPS) for s in range(HIDDEN_STEPS)]
    had = 0
    multiplied = 0
    step = 0
    for p in range(pieces):
        for d in range(1, blk_n):
            if d == min(2, last) and p + 1 < pieces:
                own_weights(p + 1)
            pass_on(p, d)
            if step < HIDDEN_STEPS:
                for c in range(had, chunk_ends[step]):
                    hidden_copy(1, c, chip, chip).wait_recv()
                    hidden_copy(2, c, chip, core).start()
                    if c + 3 < chunks:
                        hidden_copy(1, c + 3, u, chip).start()
                if p > 0:
                    if multiplied == 0:
                        for e in range(blk_n):
                            across_arrived(0, e)
                    for c in range(multiplied, had):
                        hidden_ready(c)
                        multiply((0,), c)
                    multiplied = had
                had = chunk_ends[step]
            if p == pieces - 1:
                query_chunks(d)
                if d > 1:
                    kv_pass(d - 1)
            step += 1
            if step == HIDDEN_STEPS:
                for c in range(multiplied, chunks):
                    hidden_ready(c)
                    multiply((0,), c)

                @pl.loop(0, group // PIECE)
                def _(i):
                    at = pl.ds(pl.multiple_of(i * PIECE, PIECE), PIECE)
                    kv[z, at, :HD] = turn(acc[0, at, :HD], at).astype(jnp.bfloat16)
                    kv[z, at, HD:] = acc[0, at, HD:].astype(jnp.bfloat16)

                @pl.when(z < last)
                def _():
                    kv_copy(z).start()

                query_chunks(0)

    @pl.loop(0, group // PIECE)
    def _(i):
        at = pl.ds(pl.multiple_of(i * PIECE, PIECE), PIECE)
        for p in range(1, pieces):
            for half in range(PIECE // HD):
                turned = turn(acc[p, at, half * HD : (half + 1) * HD], at)
                col = (p - 1) * PIECE + half * HD
                q_out[at, col : col + HD] = turned.astype(jnp.bfloat16)

    kv_pass(last)

    for e in range(blk_n):
        @pl.when(e <= z)
        def _(e=e):
            pltpu.make_async_copy(kv.at[e], kv_out.at[pl.ds(e * group, group)], local_sem.at[e]).start()

    for p in range(pieces):
        own_weights(p, finish=True)
        for d in range(1, blk_n):
            pass_on(p, d, finish=True)
    for c in range(chunks):
        hidden_copy(0, c, u, core).wait_send()
        hidden_copy(1, c, u, chip).wait_send()
        hidden_copy(2, c, chip, core).wait_send()
    for e in range(blk_n):
        @pl.when(e <= z)
        def _(e=e):
            @pl.when(z < last)
            def _():
                kv_copy(e).wait_send()

            pltpu.make_async_copy(kv.at[e], kv_out.at[pl.ds(e * group, group)], local_sem.at[e]).wait()


def project(hid, wq, wk, wv, cosine, sine, dp_n, blk_n, uly_n):
    tokens, width = hid.shape
    depth, query_cols = wq.shape
    chunks = dp_n * blk_n
    group = tokens * uly_n
    pieces = 1 + query_cols // PIECE
    hbm = pl.BlockSpec(memory_space=pl.ANY)
    vmem = pl.BlockSpec(memory_space=pltpu.VMEM)
    return pl.pallas_call(
        functools.partial(project_kernel, dp_n, blk_n),
        out_shape=(
            jax.ShapeDtypeStruct((group, query_cols), jnp.bfloat16),
            jax.ShapeDtypeStruct((blk_n * group, 2 * HD), jnp.bfloat16),
        ),
        in_specs=[hbm, hbm, hbm, hbm, vmem, vmem],
        out_specs=(vmem, hbm),
        scratch_shapes=[
            pltpu.VMEM((pieces, chunks, depth, PIECE), jnp.bfloat16),
            pltpu.VMEM((chunks, group, depth), jnp.bfloat16),
            pltpu.VMEM((pieces, group, PIECE), jnp.float32),
            pltpu.VMEM((blk_n, group, 2 * HD), jnp.bfloat16),
            pltpu.SemaphoreType.DMA((pieces + 1 + chunks,)),
            pltpu.SemaphoreType.DMA((pieces, 3, blk_n)),
            pltpu.SemaphoreType.DMA((pieces, chunks)),
            pltpu.SemaphoreType.DMA((3, chunks)),
            pltpu.SemaphoreType.DMA((3, chunks)),
            pltpu.SemaphoreType.DMA((blk_n,)),
            pltpu.SemaphoreType.DMA((blk_n,)),
        ],
        compiler_params=pltpu.CompilerParams(
            collective_id=0, has_side_effects=True, vmem_limit_bytes=50 * 1024 * 1024
        ),
        cost_estimate=pl.CostEstimate(
            flops=2 * group * width * (query_cols + 2 * HD), bytes_accessed=8 * 10**6, transcendentals=0
        ),
    )(hid, wq, wk, wv, cosine, sine)


def shards(hidden_states, block_table, w_query, w_key, w_value):
    tokens = hidden_states.shape[1]
    uly_size = lax.axis_size("uly")
    uly_rank = lax.axis_index("uly")
    blk_rank = lax.axis_index("blk")
    heads_here = H // uly_size
    repeats = uly_size // KV
    part_cols = HD // repeats
    query_cols = heads_here * HD
    group_rows = tokens * uly_size
    tiles = group_rows // MBLK
    dp_n, blk_n = lax.axis_size("dp"), lax.axis_size("blk")
    if dp_n == 2 and blk_n == 4 and uly_size == 4 and repeats == 1 and query_cols % PIECE == 0:
        positions = blk_rank * group_rows + jnp.arange(group_rows, dtype=jnp.int32)
        cosine, sine = angle_tables(positions)
        query, key_value = project(
            hidden_states[0],
            w_query,
            w_key,
            w_value,
            jnp.concatenate([cosine, cosine], axis=1),
            jnp.concatenate([-sine, sine], axis=1),
            dp_n,
            blk_n,
            uly_size,
        )
        result = attend(
            block_table[0], blk_rank[None].astype(jnp.int32), query, key_value, heads_here, tiles
        )
        return lax.all_to_all(result, "uly", split_axis=0, concat_axis=1, tiled=True)[None]
    w_joined = jnp.concatenate([w_query, w_key, w_value], axis=1)
    w_rows = lax.all_gather(w_joined, ("dp", "blk"), axis=0, tiled=True)
    projected = jnp.dot(
        lax.all_gather(hidden_states[0], "uly", axis=0, tiled=True),
        w_rows,
        preferred_element_type=jnp.float32,
    )
    positions = blk_rank * group_rows + jnp.arange(group_rows, dtype=jnp.int32)
    cosine, sine = angle_tables(positions)
    query = rotate(projected[:, :query_cols].reshape(group_rows, heads_here, HD), cosine, sine)
    query = query.astype(jnp.bfloat16).reshape(group_rows, query_cols)
    pieces = jnp.stack(
        [projected[:, query_cols : query_cols + part_cols], projected[:, query_cols + part_cols :]]
    )
    part_index = uly_rank % repeats
    for bit_index in range(repeats.bit_length() - 1):
        partner_piece = from_partner(pieces, "uly", bit_index)
        upper_part = part_index >> bit_index & 1 == 1
        pieces = jnp.where(
            upper_part,
            jnp.concatenate([partner_piece, pieces], axis=-1),
            jnp.concatenate([pieces, partner_piece], axis=-1),
        )
    key = rotate(pieces[0][:, None, :], cosine, sine)[:, 0, :].astype(jnp.bfloat16)
    key_value = jnp.concatenate([key, pieces[1].astype(jnp.bfloat16)], axis=1)
    key_value = lax.all_gather(key_value, "blk", axis=0, tiled=True)
    result = attend(
        block_table[0], blk_rank[None].astype(jnp.int32), query, key_value, heads_here, tiles
    )
    merged = lax.all_to_all(result, "uly", split_axis=0, concat_axis=1, tiled=True)
    return merged[None]


def solution(mesh):
    placed = (
        P("dp", ("blk", "uly"), None),
        P("dp", None, None),
        P(("dp", "blk"), "uly"),
        P(("dp", "blk"), "uly"),
        P(("dp", "blk"), "uly"),
    )
    return jax.shard_map(
        shards, mesh=mesh, in_specs=placed, out_specs=P("dp", ("blk", "uly"), None), check_vma=False
    )
```

```python
import functools

import jax
import jax.numpy as jnp
from jax import lax
from jax.experimental import pallas as pl
from jax.experimental.pallas import tpu as pltpu
from jax.sharding import PartitionSpec as P

H = 16
KV = 4
HD = 128
MBLK = 512
THETA_BASE = 500000.0
LOG2E = 1.4426950408889634
NT = (((1,), (1,)), ((), ()))
TN = (((0,), (0,)), ((), ()))


def from_partner(array, axis, distance):
    return lax.ppermute(array, axis, [(i, i ^ 1 << distance) for i in range(lax.axis_size(axis))])


def angle_tables(positions):
    half_dim = HD // 2
    exponent = jnp.arange(half_dim, dtype=jnp.float32) * (2.0 / HD)
    frequency = jnp.power(jnp.float32(THETA_BASE), -exponent)
    angles = positions.astype(jnp.float32)[:, None] * frequency[None, :]
    return jnp.cos(angles), jnp.sin(angles)


def rotate(values, cosine, sine):
    cosine, sine = cosine[:, None, :], sine[:, None, :]
    half_dim = HD // 2
    first, second = values[..., :half_dim], values[..., half_dim:]
    return jnp.concatenate([first * cosine - second * sine, second * cosine + first * sine], axis=-1)


def attend_kernel(heads, tiles, table, rank, q_ref, kv_ref, out_ref, best, total, accum):
    scale = HD**-0.5 * LOG2E

    def visit(q_start, key_block, diagonal):
        k_start = pl.multiple_of(key_block * MBLK, MBLK)
        key = kv_ref[pl.ds(k_start, MBLK), :HD]
        value = kv_ref[pl.ds(k_start, MBLK), HD:]
        for head in range(heads):
            cols = pl.ds(head * MBLK, MBLK)
            query = q_ref[pl.ds(q_start, MBLK), head * HD : (head + 1) * HD]
            scores = lax.dot_general(key, query, NT, preferred_element_type=jnp.float32) * scale
            if diagonal:
                key_at = lax.broadcasted_iota(jnp.int32, (MBLK, MBLK), 0)
                query_at = lax.broadcasted_iota(jnp.int32, (MBLK, MBLK), 1)
                scores = jnp.where(key_at <= query_at, scores, -1e30)
                new_best = jnp.max(scores, axis=0, keepdims=True)
            else:
                old_best = best[:, cols]
                new_best = jnp.maximum(old_best, jnp.max(scores, axis=0, keepdims=True))
            weights = jnp.exp2(scores - new_best)
            sums = jnp.sum(weights, axis=0, keepdims=True)
            mixed = lax.dot_general(
                value, weights.astype(jnp.bfloat16), TN, preferred_element_type=jnp.float32
            )
            best[:, cols] = new_best
            if diagonal:
                total[:, cols] = sums
                accum[:, cols] = mixed
            else:
                rescale = jnp.exp2(old_best - new_best)
                total[:, cols] = total[:, cols] * rescale + sums
                accum[:, cols] = accum[:, cols] * rescale + mixed

    for tile in range(tiles):
        q_start = tile * MBLK
        block = rank[0] * tiles + tile
        visit(q_start, block, True)

        @pl.loop(0, block)
        def _(key_block, q_start=q_start, block=block):
            @pl.when(table[block, key_block] > 0)
            def _():
                visit(q_start, key_block, False)

        for head in range(heads):
            cols = pl.ds(head * MBLK, MBLK)
            final = accum[:, cols] / total[:, cols]
            out_ref[pl.ds(q_start, MBLK), head * HD : (head + 1) * HD] = final.T.astype(jnp.bfloat16)


def attend(table, rank, query, key_value, heads, tiles):
    rows = query.shape[0]
    smem = pl.BlockSpec(memory_space=pltpu.SMEM)
    vmem = pl.BlockSpec(memory_space=pltpu.VMEM)
    return pl.pallas_call(
        functools.partial(attend_kernel, heads, tiles),
        out_shape=jax.ShapeDtypeStruct((rows, heads * HD), jnp.bfloat16),
        in_specs=[smem, smem, vmem, vmem],
        out_specs=vmem,
        scratch_shapes=[
            pltpu.VMEM((1, heads * MBLK), jnp.float32),
            pltpu.VMEM((1, heads * MBLK), jnp.float32),
            pltpu.VMEM((HD, heads * MBLK), jnp.float32),
        ],
        compiler_params=pltpu.CompilerParams(vmem_limit_bytes=48 * 1024 * 1024),
        cost_estimate=pl.CostEstimate(flops=8 * 10**9, bytes_accessed=4 * 10**6, transcendentals=16 * 10**6),
    )(table, rank, query, key_value)


PIECE = 256
MESH = pl.DeviceIdType.MESH
HIDDEN_STEPS = 6


def fused_kernel(
    dp_n, blk_n, table, hid, wq, wk, wv, cos_ref, sin_ref, out,
    weights, rows_all, acc, kv, q_rows, done, best, total, accum,
    local_sem, w_send, w_recv, h_send, h_recv, kv_send, kv_recv, o_send, o_recv,
):
    y, z, u = lax.axis_index("dp"), lax.axis_index("blk"), lax.axis_index("uly")
    last = blk_n - 1
    chunks = dp_n * blk_n
    pieces = weights.shape[0]
    tokens = hid.shape[0]
    depth = wq.shape[0]
    group = rows_all.shape[1]
    up, down, across = {"blk": z + 1}, {"blk": z - 1}, {"dp": 1 - y}
    core = u + 1 - 2 * (u % 2)
    chip = (u + 2) % 4
    far = (core + 2) % 4
    mine = y * blk_n + z

    barrier = pltpu.get_barrier_semaphore()

    @pl.when(z < last)
    def _():
        pl.semaphore_signal(barrier, inc=1, device_id=up, device_id_type=MESH)

    @pl.when(z > 0)
    def _():
        pl.semaphore_signal(barrier, inc=1, device_id=down, device_id_type=MESH)

    for where in (across, {"uly": core}, {"uly": chip}, {"uly": far}):
        pl.semaphore_signal(barrier, inc=1, device_id=where, device_id_type=MESH)

    own = [
        pltpu.make_async_copy(wk, weights.at[0, mine, :, pl.ds(0, HD)], local_sem.at[0]),
        pltpu.make_async_copy(wv, weights.at[0, mine, :, pl.ds(HD, HD)], local_sem.at[1]),
    ]
    for p in range(1, pieces):
        own.append(
            pltpu.make_async_copy(
                wq.at[:, pl.ds((p - 1) * PIECE, PIECE)], weights.at[p, mine], local_sem.at[p + 1]
            )
        )
    for c in range(chunks):
        own.append(
            pltpu.make_async_copy(
                hid.at[:, pl.ds(c * depth, depth)],
                rows_all.at[c, pl.ds(u * tokens, tokens)],
                local_sem.at[pieces + 1 + c],
            )
        )
    for copy in own:
        copy.start()
    middle = jnp.where((z > 0) & (z < last), 1, 0)
    pl.semaphore_wait(barrier, 5 + middle)

    def weight_copy(p, way, source_z, where, rank):
        return pltpu.make_async_remote_copy(
            src_ref=weights.at[p, rank], dst_ref=weights.at[p, rank],
            send_sem=w_send.at[p, way, source_z], recv_sem=w_recv.at[p, rank],
            device_id=where, device_id_type=MESH,
        )

    def hidden_copy(kind, c, source, where):
        part = rows_all.at[c, pl.ds(source * tokens, tokens)]
        return pltpu.make_async_remote_copy(
            src_ref=part, dst_ref=part, send_sem=h_send.at[kind, c], recv_sem=h_recv.at[kind, c],
            device_id={"uly": where}, device_id_type=MESH,
        )

    def kv_copy(source_z):
        return pltpu.make_async_remote_copy(
            src_ref=kv.at[source_z], dst_ref=kv.at[source_z],
            send_sem=kv_send.at[source_z], recv_sem=kv_recv.at[source_z],
            device_id=up, device_id_type=MESH,
        )

    def own_weights(p, finish=False):
        act = (lambda c: c.wait_send()) if finish else (lambda c: c.start())

        @pl.when(z < last)
        def _():
            act(weight_copy(p, 0, z, up, mine))

        @pl.when(z > 0)
        def _():
            act(weight_copy(p, 1, z, down, mine))

        act(weight_copy(p, 2, z, across, mine))

    def pass_on(p, d, finish=False):
        act = (lambda c: c.wait_send()) if finish else (lambda c: c.start())

        @pl.when(z >= d)
        def _():
            rank = y * blk_n + z - d
            if not finish:
                weight_copy(p, 0, z - d, across, rank).wait_recv()

            @pl.when(z < last)
            def _():
                act(weight_copy(p, 0, z - d, up, rank))

            act(weight_copy(p, 2, z - d, across, rank))

        @pl.when(z + d <= last)
        def _():
            rank = y * blk_n + z + d
            if not finish:
                weight_copy(p, 1, z + d, across, rank).wait_recv()

            @pl.when(z > 0)
            def _():
                act(weight_copy(p, 1, z + d, down, rank))

            act(weight_copy(p, 2, z + d, across, rank))

    def across_arrived(p, d):
        other = (1 - y) * blk_n
        if d == 0:
            weight_copy(p, 2, z, across, other + z).wait_recv()
            return

        @pl.when(z >= d)
        def _():
            weight_copy(p, 2, z - d, across, other + z - d).wait_recv()

        @pl.when(z + d <= last)
        def _():
            weight_copy(p, 2, z + d, across, other + z + d).wait_recv()

    def multiply(ps, c):
        @pl.loop(0, group // PIECE)
        def _(i):
            at = pl.ds(pl.multiple_of(i * PIECE, PIECE), PIECE)
            left = rows_all[c, at, :]
            for p in ps:
                acc[p, at, :] += jnp.dot(left, weights[p, c], preferred_element_type=jnp.float32)

    def hidden_ready(c):
        hidden_copy(0, c, core, core).wait_recv()
        hidden_copy(2, c, far, core).wait_recv()

    def turn(values, at):
        return values * cos_ref[at, :] + pltpu.roll(values, HD // 2, 1) * sin_ref[at, :]

    def query_chunks(d):
        for p in range(1, pieces):
            across_arrived(p, d)
        ps = tuple(range(1, pieces))
        if d == 0:
            multiply(ps, mine)
            multiply(ps, (1 - y) * blk_n + z)
            return

        @pl.when(z >= d)
        def _():
            multiply(ps, y * blk_n + z - d)
            multiply(ps, (1 - y) * blk_n + z - d)

        @pl.when(z + d <= last)
        def _():
            multiply(ps, y * blk_n + z + d)
            multiply(ps, (1 - y) * blk_n + z + d)

    def kv_pass(d):
        @pl.when(z >= d)
        def _():
            kv_copy(z - d).wait_recv()

            @pl.when(z < last)
            def _():
                kv_copy(z - d).start()

    own[0].wait()
    own[1].wait()
    own_weights(0)
    for c in range(chunks):
        own[pieces + 1 + c].wait()
        if c < 3:
            hidden_copy(1, c, u, chip).start()
    for c in range(chunks):
        hidden_copy(0, c, u, core).start()
    for p in range(1, pieces):
        own[p + 1].wait()
    acc[...] = jnp.zeros_like(acc)

    chunk_ends = [-(-chunks * (s + 1) // HIDDEN_STEPS) for s in range(HIDDEN_STEPS)]
    had = 0
    multiplied = 0
    step = 0
    for p in range(pieces):
        for d in range(1, blk_n):
            if d == 1 and p + 1 < pieces:
                own_weights(p + 1)
            pass_on(p, d)
            if step < HIDDEN_STEPS:
                for c in range(had, chunk_ends[step]):
                    hidden_copy(1, c, chip, chip).wait_recv()
                    hidden_copy(2, c, chip, core).start()
                    if c + 3 < chunks:
                        hidden_copy(1, c + 3, u, chip).start()
                if p > 0:
                    if multiplied == 0:
                        for e in range(blk_n):
                            across_arrived(0, e)
                    for c in range(multiplied, had):
                        hidden_ready(c)
                        multiply((0,), c)
                    multiplied = had
                had = chunk_ends[step]
            if p == pieces - 1:
                query_chunks(d)
                if d > 1:
                    kv_pass(d - 1)
            step += 1
            if step == HIDDEN_STEPS:
                for c in range(multiplied, chunks):
                    hidden_ready(c)
                    multiply((0,), c)

                @pl.loop(0, group // PIECE)
                def _(i):
                    at = pl.ds(pl.multiple_of(i * PIECE, PIECE), PIECE)
                    kv[z, at, :HD] = turn(acc[0, at, :HD], at).astype(jnp.bfloat16)
                    kv[z, at, HD:] = acc[0, at, HD:].astype(jnp.bfloat16)

                @pl.when(z < last)
                def _():
                    kv_copy(z).start()

                query_chunks(0)

    @pl.loop(0, group // PIECE)
    def _(i):
        at = pl.ds(pl.multiple_of(i * PIECE, PIECE), PIECE)
        for p in range(1, pieces):
            for half in range(PIECE // HD):
                turned = turn(acc[p, at, half * HD : (half + 1) * HD], at)
                col = (p - 1) * PIECE + half * HD
                q_rows[at, col : col + HD] = turned.astype(jnp.bfloat16)

    scale = HD**-0.5 * LOG2E
    tiles = group // MBLK
    heads = q_rows.shape[1] // HD
    query_cols = q_rows.shape[1]

    def visit(q_tile, source_z, k_tile, first):
        keys = kv.at[source_z, pl.ds(pl.multiple_of(k_tile * MBLK, MBLK), MBLK)]
        key, value = keys[:, :HD], keys[:, HD:]
        q_at = pl.ds(pl.multiple_of(q_tile * MBLK, MBLK), MBLK)
        allowed = table[z * tiles + q_tile, source_z * tiles + k_tile]
        bias = jnp.where(allowed > 0, 0.0, -1e30).astype(jnp.float32)
        for head in range(heads):
            cols = slice(head * MBLK, (head + 1) * MBLK)
            query = q_rows[q_at, head * HD : (head + 1) * HD]
            scores = lax.dot_general(key, query, NT, preferred_element_type=jnp.float32) * scale
            if first:
                key_at = lax.broadcasted_iota(jnp.int32, (MBLK, MBLK), 0)
                query_at = lax.broadcasted_iota(jnp.int32, (MBLK, MBLK), 1)
                scores = jnp.where(key_at <= query_at, scores, -1e30)
                new_best = jnp.max(scores, axis=0, keepdims=True)
            else:
                scores = scores + bias
                old_best = best[q_tile, :, cols]
                new_best = jnp.maximum(old_best, jnp.max(scores, axis=0, keepdims=True))
            grown = jnp.exp2(scores - new_best)
            sums = jnp.sum(grown, axis=0, keepdims=True)
            mixed = lax.dot_general(
                value, grown.astype(jnp.bfloat16), TN, preferred_element_type=jnp.float32
            )
            best[q_tile, :, cols] = new_best
            if first:
                total[q_tile, :, cols] = sums
                accum[q_tile, :, cols] = mixed
            else:
                rescale = jnp.exp2(old_best - new_best)
                total[q_tile, :, cols] = total[q_tile, :, cols] * rescale + sums
                accum[q_tile, :, cols] = accum[q_tile, :, cols] * rescale + mixed

    def out_copy(owner):
        return pltpu.make_async_remote_copy(
            src_ref=done.at[pl.ds(owner * tokens, tokens)],
            dst_ref=out.at[:, pl.ds(pl.multiple_of(u * query_cols, query_cols), query_cols)],
            send_sem=o_send.at[owner], recv_sem=o_recv.at[u],
            device_id={"uly": owner}, device_id_type=MESH,
        )

    def out_arrival(source):
        return pltpu.make_async_remote_copy(
            src_ref=done.at[pl.ds(source * tokens, tokens)],
            dst_ref=out.at[:, pl.ds(pl.multiple_of(source * query_cols, query_cols), query_cols)],
            send_sem=o_send.at[source], recv_sem=o_recv.at[source],
            device_id={"uly": source}, device_id_type=MESH,
        )

    def out_own():
        return pltpu.make_async_copy(
            done.at[pl.ds(u * tokens, tokens)],
            out.at[:, pl.ds(pl.multiple_of(u * query_cols, query_cols), query_cols)],
            local_sem.at[0],
        )

    def finalize(q_tile):
        q_at = pl.ds(pl.multiple_of(q_tile * MBLK, MBLK), MBLK)
        for head in range(heads):
            cols = slice(head * MBLK, (head + 1) * MBLK)
            final = accum[q_tile, :, cols] / total[q_tile, :, cols]
            done[q_at, head * HD : (head + 1) * HD] = final.T.astype(jnp.bfloat16)
        owners = MBLK // tokens
        for e in range(owners):
            owner = q_tile * owners + e

            @pl.when(owner != u)
            def _():
                out_copy(owner).start()

            @pl.when(owner == u)
            def _():
                out_own().start()

    @pl.loop(0, tiles)
    def _(q_tile):
        visit(q_tile, z, q_tile, True)

        @pl.loop(0, q_tile)
        def _(k_tile):
            visit(q_tile, z, k_tile, False)

        @pl.when(z == 0)
        def _():
            finalize(q_tile)

    for d in range(1, blk_n):
        if d == last:
            kv_pass(d)

        @pl.when(z >= d)
        def _(d=d):
            @pl.loop(0, tiles)
            def _(q_tile):
                @pl.loop(0, tiles)
                def _(k_tile):
                    visit(q_tile, z - d, k_tile, False)

                @pl.when(z == d)
                def _():
                    finalize(q_tile)

    for p in range(pieces):
        own_weights(p, finish=True)
        for d in range(1, blk_n):
            pass_on(p, d, finish=True)
    for c in range(chunks):
        hidden_copy(0, c, u, core).wait_send()
        hidden_copy(1, c, u, chip).wait_send()
        hidden_copy(2, c, chip, core).wait_send()
    for e in range(blk_n):
        @pl.when(e <= z)
        def _(e=e):
            @pl.when(z < last)
            def _():
                kv_copy(e).wait_send()

    out_own().wait()
    for other in (core, chip, far):
        out_copy(other).wait_send()
        out_arrival(other).wait_recv()


def fused(table, hid, wq, wk, wv, cosine, sine, dp_n, blk_n, uly_n):
    tokens, width = hid.shape
    depth, query_cols = wq.shape
    chunks = dp_n * blk_n
    group = tokens * uly_n
    pieces = 1 + query_cols // PIECE
    tiles, heads = group // MBLK, query_cols // HD
    hbm = pl.BlockSpec(memory_space=pl.ANY)
    vmem = pl.BlockSpec(memory_space=pltpu.VMEM)
    return pl.pallas_call(
        functools.partial(fused_kernel, dp_n, blk_n),
        out_shape=jax.ShapeDtypeStruct((tokens, uly_n * query_cols), jnp.bfloat16),
        in_specs=[pl.BlockSpec(memory_space=pltpu.SMEM), hbm, hbm, hbm, hbm, vmem, vmem],
        out_specs=hbm,
        scratch_shapes=[
            pltpu.VMEM((pieces, chunks, depth, PIECE), jnp.bfloat16),
            pltpu.VMEM((chunks, group, depth), jnp.bfloat16),
            pltpu.VMEM((pieces, group, PIECE), jnp.float32),
            pltpu.VMEM((blk_n, group, 2 * HD), jnp.bfloat16),
            pltpu.VMEM((group, query_cols), jnp.bfloat16),
            pltpu.VMEM((group, query_cols), jnp.bfloat16),
            pltpu.VMEM((tiles, 1, heads * MBLK), jnp.float32),
            pltpu.VMEM((tiles, 1, heads * MBLK), jnp.float32),
            pltpu.VMEM((tiles, HD, heads * MBLK), jnp.float32),
            pltpu.SemaphoreType.DMA((pieces + 1 + chunks,)),
            pltpu.SemaphoreType.DMA((pieces, 3, blk_n)),
            pltpu.SemaphoreType.DMA((pieces, chunks)),
            pltpu.SemaphoreType.DMA((3, chunks)),
            pltpu.SemaphoreType.DMA((3, chunks)),
            pltpu.SemaphoreType.DMA((blk_n,)),
            pltpu.SemaphoreType.DMA((blk_n,)),
            pltpu.SemaphoreType.DMA((uly_n,)),
            pltpu.SemaphoreType.DMA((uly_n,)),
        ],
        compiler_params=pltpu.CompilerParams(
            collective_id=0, has_side_effects=True, vmem_limit_bytes=50 * 1024 * 1024
        ),
        cost_estimate=pl.CostEstimate(
            flops=2 * group * width * (query_cols + 2 * HD), bytes_accessed=8 * 10**6, transcendentals=0
        ),
    )(table, hid, wq, wk, wv, cosine, sine)


def shards(hidden_states, block_table, w_query, w_key, w_value):
    tokens = hidden_states.shape[1]
    uly_size = lax.axis_size("uly")
    uly_rank = lax.axis_index("uly")
    blk_rank = lax.axis_index("blk")
    heads_here = H // uly_size
    repeats = uly_size // KV
    part_cols = HD // repeats
    query_cols = heads_here * HD
    group_rows = tokens * uly_size
    tiles = group_rows // MBLK
    dp_n, blk_n = lax.axis_size("dp"), lax.axis_size("blk")
    if dp_n == 2 and blk_n == 4 and uly_size == 4 and repeats == 1 and query_cols % PIECE == 0:
        positions = blk_rank * group_rows + jnp.arange(group_rows, dtype=jnp.int32)
        cosine, sine = angle_tables(positions)
        merged = fused(
            block_table[0],
            hidden_states[0],
            w_query,
            w_key,
            w_value,
            jnp.concatenate([cosine, cosine], axis=1),
            jnp.concatenate([-sine, sine], axis=1),
            dp_n,
            blk_n,
            uly_size,
        )
        return merged[None]
    w_joined = jnp.concatenate([w_query, w_key, w_value], axis=1)
    w_rows = lax.all_gather(w_joined, ("dp", "blk"), axis=0, tiled=True)
    projected = jnp.dot(
        lax.all_gather(hidden_states[0], "uly", axis=0, tiled=True),
        w_rows,
        preferred_element_type=jnp.float32,
    )
    positions = blk_rank * group_rows + jnp.arange(group_rows, dtype=jnp.int32)
    cosine, sine = angle_tables(positions)
    query = rotate(projected[:, :query_cols].reshape(group_rows, heads_here, HD), cosine, sine)
    query = query.astype(jnp.bfloat16).reshape(group_rows, query_cols)
    pieces = jnp.stack(
        [projected[:, query_cols : query_cols + part_cols], projected[:, query_cols + part_cols :]]
    )
    part_index = uly_rank % repeats
    for bit_index in range(repeats.bit_length() - 1):
        partner_piece = from_partner(pieces, "uly", bit_index)
        upper_part = part_index >> bit_index & 1 == 1
        pieces = jnp.where(
            upper_part,
            jnp.concatenate([partner_piece, pieces], axis=-1),
            jnp.concatenate([pieces, partner_piece], axis=-1),
        )
    key = rotate(pieces[0][:, None, :], cosine, sine)[:, 0, :].astype(jnp.bfloat16)
    key_value = jnp.concatenate([key, pieces[1].astype(jnp.bfloat16)], axis=1)
    key_value = lax.all_gather(key_value, "blk", axis=0, tiled=True)
    result = attend(
        block_table[0], blk_rank[None].astype(jnp.int32), query, key_value, heads_here, tiles
    )
    merged = lax.all_to_all(result, "uly", split_axis=0, concat_axis=1, tiled=True)
    return merged[None]


def solution(mesh):
    placed = (
        P("dp", ("blk", "uly"), None),
        P("dp", None, None),
        P(("dp", "blk"), "uly"),
        P(("dp", "blk"), "uly"),
        P(("dp", "blk"), "uly"),
    )
    return jax.shard_map(
        shards, mesh=mesh, in_specs=placed, out_specs=P("dp", ("blk", "uly"), None), check_vma=False
    )
```

```python
import functools

import jax
import jax.numpy as jnp
from jax import lax
from jax.experimental import pallas as pl
from jax.experimental.pallas import tpu as pltpu
from jax.sharding import PartitionSpec as P

H = 16
KV = 4
HD = 128
MBLK = 512
THETA_BASE = 500000.0
LOG2E = 1.4426950408889634
NT = (((1,), (1,)), ((), ()))
TN = (((0,), (0,)), ((), ()))


def from_partner(array, axis, distance):
    return lax.ppermute(array, axis, [(i, i ^ 1 << distance) for i in range(lax.axis_size(axis))])


def angle_tables(positions):
    half_dim = HD // 2
    exponent = jnp.arange(half_dim, dtype=jnp.float32) * (2.0 / HD)
    frequency = jnp.power(jnp.float32(THETA_BASE), -exponent)
    angles = positions.astype(jnp.float32)[:, None] * frequency[None, :]
    return jnp.cos(angles), jnp.sin(angles)


def rotate(values, cosine, sine):
    cosine, sine = cosine[:, None, :], sine[:, None, :]
    half_dim = HD // 2
    first, second = values[..., :half_dim], values[..., half_dim:]
    return jnp.concatenate([first * cosine - second * sine, second * cosine + first * sine], axis=-1)


def attend_kernel(heads, tiles, table, rank, q_ref, kv_ref, out_ref, best, total, accum):
    scale = HD**-0.5 * LOG2E

    def visit(q_start, key_block, diagonal):
        k_start = pl.multiple_of(key_block * MBLK, MBLK)
        key = kv_ref[pl.ds(k_start, MBLK), :HD]
        value = kv_ref[pl.ds(k_start, MBLK), HD:]
        for head in range(heads):
            cols = pl.ds(head * MBLK, MBLK)
            query = q_ref[pl.ds(q_start, MBLK), head * HD : (head + 1) * HD]
            scores = lax.dot_general(key, query, NT, preferred_element_type=jnp.float32) * scale
            if diagonal:
                key_at = lax.broadcasted_iota(jnp.int32, (MBLK, MBLK), 0)
                query_at = lax.broadcasted_iota(jnp.int32, (MBLK, MBLK), 1)
                scores = jnp.where(key_at <= query_at, scores, -1e30)
                new_best = jnp.max(scores, axis=0, keepdims=True)
            else:
                old_best = best[:, cols]
                new_best = jnp.maximum(old_best, jnp.max(scores, axis=0, keepdims=True))
            weights = jnp.exp2(scores - new_best)
            sums = jnp.sum(weights, axis=0, keepdims=True)
            mixed = lax.dot_general(
                value, weights.astype(jnp.bfloat16), TN, preferred_element_type=jnp.float32
            )
            best[:, cols] = new_best
            if diagonal:
                total[:, cols] = sums
                accum[:, cols] = mixed
            else:
                rescale = jnp.exp2(old_best - new_best)
                total[:, cols] = total[:, cols] * rescale + sums
                accum[:, cols] = accum[:, cols] * rescale + mixed

    for tile in range(tiles):
        q_start = tile * MBLK
        block = rank[0] * tiles + tile
        visit(q_start, block, True)

        @pl.loop(0, block)
        def _(key_block, q_start=q_start, block=block):
            @pl.when(table[block, key_block] > 0)
            def _():
                visit(q_start, key_block, False)

        for head in range(heads):
            cols = pl.ds(head * MBLK, MBLK)
            final = accum[:, cols] / total[:, cols]
            out_ref[pl.ds(q_start, MBLK), head * HD : (head + 1) * HD] = final.T.astype(jnp.bfloat16)


def attend(table, rank, query, key_value, heads, tiles):
    rows = query.shape[0]
    smem = pl.BlockSpec(memory_space=pltpu.SMEM)
    vmem = pl.BlockSpec(memory_space=pltpu.VMEM)
    return pl.pallas_call(
        functools.partial(attend_kernel, heads, tiles),
        out_shape=jax.ShapeDtypeStruct((rows, heads * HD), jnp.bfloat16),
        in_specs=[smem, smem, vmem, vmem],
        out_specs=vmem,
        scratch_shapes=[
            pltpu.VMEM((1, heads * MBLK), jnp.float32),
            pltpu.VMEM((1, heads * MBLK), jnp.float32),
            pltpu.VMEM((HD, heads * MBLK), jnp.float32),
        ],
        compiler_params=pltpu.CompilerParams(vmem_limit_bytes=48 * 1024 * 1024),
        cost_estimate=pl.CostEstimate(flops=8 * 10**9, bytes_accessed=4 * 10**6, transcendentals=16 * 10**6),
    )(table, rank, query, key_value)


PIECE = 256
MESH = pl.DeviceIdType.MESH
IN_FLIGHT = 4


def fused_kernel(
    dp_n, blk_n, table, hid, wq, wk, wv, cos_ref, sin_ref, out,
    weights, rows_all, acc, kv, q_rows, done, best, total, accum,
    local_sem, w_send, w_recv, h_send, h_recv, kv_send, kv_recv, o_send, o_recv,
):
    y, z, u = lax.axis_index("dp"), lax.axis_index("blk"), lax.axis_index("uly")
    last = blk_n - 1
    chunks = dp_n * blk_n
    pieces = weights.shape[0]
    tokens = hid.shape[0]
    depth = wq.shape[0]
    group = rows_all.shape[1]
    up, down, across = {"blk": z + 1}, {"blk": z - 1}, {"dp": 1 - y}
    core = u + 1 - 2 * (u % 2)
    chip = (u + 2) % 4
    far = (core + 2) % 4
    mine = y * blk_n + z

    barrier = pltpu.get_barrier_semaphore()

    @pl.when(z < last)
    def _():
        pl.semaphore_signal(barrier, inc=1, device_id=up, device_id_type=MESH)

    @pl.when(z > 0)
    def _():
        pl.semaphore_signal(barrier, inc=1, device_id=down, device_id_type=MESH)

    for where in (across, {"uly": core}, {"uly": chip}, {"uly": far}):
        pl.semaphore_signal(barrier, inc=1, device_id=where, device_id_type=MESH)

    own = [
        pltpu.make_async_copy(wk, weights.at[0, mine, :, pl.ds(0, HD)], local_sem.at[0]),
        pltpu.make_async_copy(wv, weights.at[0, mine, :, pl.ds(HD, HD)], local_sem.at[1]),
    ]
    for p in range(1, pieces):
        own.append(
            pltpu.make_async_copy(
                wq.at[:, pl.ds((p - 1) * PIECE, PIECE)], weights.at[p, mine], local_sem.at[p + 1]
            )
        )
    for c in range(chunks):
        own.append(
            pltpu.make_async_copy(
                hid.at[:, pl.ds(c * depth, depth)],
                rows_all.at[c, pl.ds(u * tokens, tokens)],
                local_sem.at[pieces + 1 + c],
            )
        )
    for copy in own:
        copy.start()
    middle = jnp.where((z > 0) & (z < last), 1, 0)
    pl.semaphore_wait(barrier, 5 + middle)

    def weight_copy(p, way, source_z, where, rank):
        return pltpu.make_async_remote_copy(
            src_ref=weights.at[p, rank], dst_ref=weights.at[p, rank],
            send_sem=w_send.at[p, way, source_z], recv_sem=w_recv.at[p, rank],
            device_id=where, device_id_type=MESH,
        )

    def hidden_copy(kind, c, source, where):
        part = rows_all.at[c, pl.ds(source * tokens, tokens)]
        return pltpu.make_async_remote_copy(
            src_ref=part, dst_ref=part, send_sem=h_send.at[kind, c], recv_sem=h_recv.at[kind, c],
            device_id={"uly": where}, device_id_type=MESH,
        )

    own_tile = u // 2

    def tile_rows(half):
        tile = own_tile if half == 0 else 1 - own_tile
        return pl.multiple_of(tile * MBLK, MBLK)

    def kv_copy(source_z, half):
        part = kv.at[source_z, pl.ds(tile_rows(half), MBLK)]
        return pltpu.make_async_remote_copy(
            src_ref=part, dst_ref=part,
            send_sem=kv_send.at[half, source_z], recv_sem=kv_recv.at[half, source_z],
            device_id=up, device_id_type=MESH,
        )

    def own_weights(p, finish=False):
        act = (lambda c: c.wait_send()) if finish else (lambda c: c.start())

        @pl.when(z < last)
        def _():
            act(weight_copy(p, 0, z, up, mine))

        @pl.when(z > 0)
        def _():
            act(weight_copy(p, 1, z, down, mine))

        act(weight_copy(p, 2, z, across, mine))

    def pass_on(p, d, finish=False):
        act = (lambda c: c.wait_send()) if finish else (lambda c: c.start())

        @pl.when(z >= d)
        def _():
            rank = y * blk_n + z - d
            if not finish:
                weight_copy(p, 0, z - d, across, rank).wait_recv()

            @pl.when(z < last)
            def _():
                act(weight_copy(p, 0, z - d, up, rank))

            act(weight_copy(p, 2, z - d, across, rank))

        @pl.when(z + d <= last)
        def _():
            rank = y * blk_n + z + d
            if not finish:
                weight_copy(p, 1, z + d, across, rank).wait_recv()

            @pl.when(z > 0)
            def _():
                act(weight_copy(p, 1, z + d, down, rank))

            act(weight_copy(p, 2, z + d, across, rank))

    def across_arrived(p, d):
        other = (1 - y) * blk_n
        if d == 0:
            weight_copy(p, 2, z, across, other + z).wait_recv()
            return

        @pl.when(z >= d)
        def _():
            weight_copy(p, 2, z - d, across, other + z - d).wait_recv()

        @pl.when(z + d <= last)
        def _():
            weight_copy(p, 2, z + d, across, other + z + d).wait_recv()

    def multiply(c):
        @pl.loop(0, group // PIECE)
        def _(i):
            at = pl.ds(pl.multiple_of(i * PIECE, PIECE), PIECE)
            acc[at, :] += jnp.dot(
                rows_all[c, at, :], weights[pieces - 1, c], preferred_element_type=jnp.float32
            )

    def whole_sum(p, at):
        result = jnp.dot(rows_all[0, at, :], weights[p, 0], preferred_element_type=jnp.float32)
        for c in range(1, chunks):
            result += jnp.dot(rows_all[c, at, :], weights[p, c], preferred_element_type=jnp.float32)
        return result

    def turn(values, at):
        return values * cos_ref[at, :] + pltpu.roll(values, HD // 2, 1) * sin_ref[at, :]

    def kv_half(half):
        @pl.loop(0, MBLK // PIECE)
        def _(i):
            at = pl.ds(pl.multiple_of(tile_rows(half) + i * PIECE, PIECE), PIECE)
            both = whole_sum(0, at)
            kv[z, at, :HD] = turn(both[:, :HD], at).astype(jnp.bfloat16)
            kv[z, at, HD:] = both[:, HD:].astype(jnp.bfloat16)

        @pl.when(z < last)
        def _():
            kv_copy(z, half).start()

    def keep_query(p, at, values):
        for half in range(PIECE // HD):
            col = (p - 1) * PIECE + half * HD
            turned = turn(values[:, half * HD : (half + 1) * HD], at)
            q_rows[at, col : col + HD] = turned.astype(jnp.bfloat16)

    def whole_queries(lower, upper):
        @pl.loop(lower, upper)
        def _(i):
            at = pl.ds(pl.multiple_of(i * PIECE, PIECE), PIECE)
            for p in range(1, pieces - 1):
                keep_query(p, at, whole_sum(p, at))

    def query_chunks(d):
        across_arrived(pieces - 1, d)
        if d == 0:
            multiply(mine)
            multiply((1 - y) * blk_n + z)
            return

        @pl.when(z >= d)
        def _():
            multiply(y * blk_n + z - d)
            multiply((1 - y) * blk_n + z - d)

        @pl.when(z + d <= last)
        def _():
            multiply(y * blk_n + z + d)
            multiply((1 - y) * blk_n + z + d)

    def kv_pass(d, half):
        @pl.when(z >= d)
        def _():
            kv_copy(z - d, half).wait_recv()

            @pl.when(z < last)
            def _():
                kv_copy(z - d, half).start()

    def hidden_step(lower, upper):
        for c in range(lower, upper):
            hidden_copy(1, c, chip, chip).wait_recv()
            hidden_copy(2, c, chip, core).start()
            if c + IN_FLIGHT < chunks:
                hidden_copy(1, c + IN_FLIGHT, u, chip).start()

    own[0].wait()
    own[1].wait()
    own_weights(0)
    for c in range(chunks):
        own[pieces + 1 + c].wait()
        if c < IN_FLIGHT:
            hidden_copy(1, c, u, chip).start()
    for c in range(chunks):
        hidden_copy(0, c, u, core).start()
    for p in range(1, pieces):
        own[p + 1].wait()
    acc[...] = jnp.zeros_like(acc)

    slabs = group // PIECE
    ends = (0, 1, 3, 5, 7, 8)
    step = 0
    for p in range(pieces):
        for d in range(1, blk_n):
            if d == 1 and p + 1 < pieces:
                own_weights(p + 1)
            pass_on(p, d)
            if 0 < step < len(ends):
                hidden_step(ends[step - 1], ends[step])
            if step == 3:
                for e in range(blk_n):
                    across_arrived(0, e)
                for c in range(chunks):
                    hidden_copy(0, c, core, core).wait_recv()
                kv_half(0)
            elif step == 5:
                kv_pass(1, 0)
                for c in range(chunks):
                    hidden_copy(2, c, far, core).wait_recv()
                kv_half(1)
            elif step == 6:
                query_chunks(0)
            elif step == 7:
                kv_pass(2, 0)
                kv_pass(1, 1)
                for e in range(blk_n):
                    across_arrived(1, e)
                whole_queries(0, slabs // 2)
                query_chunks(1)
            elif step == 8:
                whole_queries(slabs // 2, slabs)
                query_chunks(2)
                kv_pass(2, 1)
                query_chunks(3)
            step += 1

    @pl.loop(0, slabs)
    def _(i):
        at = pl.ds(pl.multiple_of(i * PIECE, PIECE), PIECE)
        keep_query(pieces - 1, at, acc[at, :])

    scale = HD**-0.5 * LOG2E
    tiles = group // MBLK
    heads = q_rows.shape[1] // HD
    query_cols = q_rows.shape[1]

    def visit(q_tile, source_z, k_tile, first):
        keys = kv.at[source_z, pl.ds(pl.multiple_of(k_tile * MBLK, MBLK), MBLK)]
        key, value = keys[:, :HD], keys[:, HD:]
        q_at = pl.ds(pl.multiple_of(q_tile * MBLK, MBLK), MBLK)
        allowed = table[z * tiles + q_tile, source_z * tiles + k_tile]
        bias = jnp.where(allowed > 0, 0.0, -1e30).astype(jnp.float32)
        for head in range(heads):
            cols = slice(head * MBLK, (head + 1) * MBLK)
            query = q_rows[q_at, head * HD : (head + 1) * HD]
            scores = lax.dot_general(key, query, NT, preferred_element_type=jnp.float32) * scale
            if first:
                key_at = lax.broadcasted_iota(jnp.int32, (MBLK, MBLK), 0)
                query_at = lax.broadcasted_iota(jnp.int32, (MBLK, MBLK), 1)
                scores = jnp.where(key_at <= query_at, scores, -1e30)
                new_best = jnp.max(scores, axis=0, keepdims=True)
            else:
                scores = scores + bias
                old_best = best[q_tile, :, cols]
                new_best = jnp.maximum(old_best, jnp.max(scores, axis=0, keepdims=True))
            grown = jnp.exp2(scores - new_best)
            sums = jnp.sum(grown, axis=0, keepdims=True)
            mixed = lax.dot_general(
                value, grown.astype(jnp.bfloat16), TN, preferred_element_type=jnp.float32
            )
            best[q_tile, :, cols] = new_best
            if first:
                total[q_tile, :, cols] = sums
                accum[q_tile, :, cols] = mixed
            else:
                rescale = jnp.exp2(old_best - new_best)
                total[q_tile, :, cols] = total[q_tile, :, cols] * rescale + sums
                accum[q_tile, :, cols] = accum[q_tile, :, cols] * rescale + mixed

    def out_copy(owner):
        return pltpu.make_async_remote_copy(
            src_ref=done.at[pl.ds(owner * tokens, tokens)],
            dst_ref=out.at[:, pl.ds(pl.multiple_of(u * query_cols, query_cols), query_cols)],
            send_sem=o_send.at[owner], recv_sem=o_recv.at[u],
            device_id={"uly": owner}, device_id_type=MESH,
        )

    def out_arrival(source):
        return pltpu.make_async_remote_copy(
            src_ref=done.at[pl.ds(source * tokens, tokens)],
            dst_ref=out.at[:, pl.ds(pl.multiple_of(source * query_cols, query_cols), query_cols)],
            send_sem=o_send.at[source], recv_sem=o_recv.at[source],
            device_id={"uly": source}, device_id_type=MESH,
        )

    def out_own():
        return pltpu.make_async_copy(
            done.at[pl.ds(u * tokens, tokens)],
            out.at[:, pl.ds(pl.multiple_of(u * query_cols, query_cols), query_cols)],
            local_sem.at[0],
        )

    def finalize(q_tile):
        q_at = pl.ds(pl.multiple_of(q_tile * MBLK, MBLK), MBLK)
        for head in range(heads):
            cols = slice(head * MBLK, (head + 1) * MBLK)
            final = accum[q_tile, :, cols] / total[q_tile, :, cols]
            done[q_at, head * HD : (head + 1) * HD] = final.T.astype(jnp.bfloat16)
        owners = MBLK // tokens
        for e in range(owners):
            owner = q_tile * owners + e

            @pl.when(owner != u)
            def _():
                out_copy(owner).start()

            @pl.when(owner == u)
            def _():
                out_own().start()

    @pl.loop(0, tiles)
    def _(q_tile):
        visit(q_tile, z, q_tile, True)

        @pl.loop(0, q_tile)
        def _(k_tile):
            visit(q_tile, z, k_tile, False)

        @pl.when(z == 0)
        def _():
            finalize(q_tile)

    for d in range(1, blk_n):
        if d == last:
            kv_pass(d, 0)
            kv_pass(d, 1)

        @pl.when(z >= d)
        def _(d=d):
            @pl.loop(0, tiles)
            def _(q_tile):
                @pl.loop(0, tiles)
                def _(k_tile):
                    visit(q_tile, z - d, k_tile, False)

                @pl.when(z == d)
                def _():
                    finalize(q_tile)

    for p in range(pieces):
        own_weights(p, finish=True)
        for d in range(1, blk_n):
            pass_on(p, d, finish=True)
    for c in range(chunks):
        hidden_copy(0, c, u, core).wait_send()
        hidden_copy(1, c, u, chip).wait_send()
        hidden_copy(2, c, chip, core).wait_send()
    for e in range(blk_n):
        @pl.when(e <= z)
        def _(e=e):
            @pl.when(z < last)
            def _():
                kv_copy(e, 0).wait_send()
                kv_copy(e, 1).wait_send()

    out_own().wait()
    for other in (core, chip, far):
        out_copy(other).wait_send()
        out_arrival(other).wait_recv()


def fused(table, hid, wq, wk, wv, cosine, sine, dp_n, blk_n, uly_n):
    tokens, width = hid.shape
    depth, query_cols = wq.shape
    chunks = dp_n * blk_n
    group = tokens * uly_n
    pieces = 1 + query_cols // PIECE
    tiles, heads = group // MBLK, query_cols // HD
    hbm = pl.BlockSpec(memory_space=pl.ANY)
    vmem = pl.BlockSpec(memory_space=pltpu.VMEM)
    return pl.pallas_call(
        functools.partial(fused_kernel, dp_n, blk_n),
        out_shape=jax.ShapeDtypeStruct((tokens, uly_n * query_cols), jnp.bfloat16),
        in_specs=[pl.BlockSpec(memory_space=pltpu.SMEM), hbm, hbm, hbm, hbm, vmem, vmem],
        out_specs=hbm,
        scratch_shapes=[
            pltpu.VMEM((pieces, chunks, depth, PIECE), jnp.bfloat16),
            pltpu.VMEM((chunks, group, depth), jnp.bfloat16),
            pltpu.VMEM((group, PIECE), jnp.float32),
            pltpu.VMEM((blk_n, group, 2 * HD), jnp.bfloat16),
            pltpu.VMEM((group, query_cols), jnp.bfloat16),
            pltpu.VMEM((group, query_cols), jnp.bfloat16),
            pltpu.VMEM((tiles, 1, heads * MBLK), jnp.float32),
            pltpu.VMEM((tiles, 1, heads * MBLK), jnp.float32),
            pltpu.VMEM((tiles, HD, heads * MBLK), jnp.float32),
            pltpu.SemaphoreType.DMA((pieces + 1 + chunks,)),
            pltpu.SemaphoreType.DMA((pieces, 3, blk_n)),
            pltpu.SemaphoreType.DMA((pieces, chunks)),
            pltpu.SemaphoreType.DMA((3, chunks)),
            pltpu.SemaphoreType.DMA((3, chunks)),
            pltpu.SemaphoreType.DMA((2, blk_n)),
            pltpu.SemaphoreType.DMA((2, blk_n)),
            pltpu.SemaphoreType.DMA((uly_n,)),
            pltpu.SemaphoreType.DMA((uly_n,)),
        ],
        compiler_params=pltpu.CompilerParams(
            collective_id=0, has_side_effects=True, vmem_limit_bytes=50 * 1024 * 1024
        ),
        cost_estimate=pl.CostEstimate(
            flops=2 * group * width * (query_cols + 2 * HD), bytes_accessed=8 * 10**6, transcendentals=0
        ),
    )(table, hid, wq, wk, wv, cosine, sine)


def shards(hidden_states, block_table, w_query, w_key, w_value):
    tokens = hidden_states.shape[1]
    uly_size = lax.axis_size("uly")
    uly_rank = lax.axis_index("uly")
    blk_rank = lax.axis_index("blk")
    heads_here = H // uly_size
    repeats = uly_size // KV
    part_cols = HD // repeats
    query_cols = heads_here * HD
    group_rows = tokens * uly_size
    tiles = group_rows // MBLK
    dp_n, blk_n = lax.axis_size("dp"), lax.axis_size("blk")
    if dp_n == 2 and blk_n == 4 and uly_size == 4 and repeats == 1 and query_cols == 2 * PIECE and tokens * 2 == MBLK:
        positions = blk_rank * group_rows + jnp.arange(group_rows, dtype=jnp.int32)
        cosine, sine = angle_tables(positions)
        merged = fused(
            block_table[0],
            hidden_states[0],
            w_query,
            w_key,
            w_value,
            jnp.concatenate([cosine, cosine], axis=1),
            jnp.concatenate([-sine, sine], axis=1),
            dp_n,
            blk_n,
            uly_size,
        )
        return merged[None]
    w_joined = jnp.concatenate([w_query, w_key, w_value], axis=1)
    w_rows = lax.all_gather(w_joined, ("dp", "blk"), axis=0, tiled=True)
    projected = jnp.dot(
        lax.all_gather(hidden_states[0], "uly", axis=0, tiled=True),
        w_rows,
        preferred_element_type=jnp.float32,
    )
    positions = blk_rank * group_rows + jnp.arange(group_rows, dtype=jnp.int32)
    cosine, sine = angle_tables(positions)
    query = rotate(projected[:, :query_cols].reshape(group_rows, heads_here, HD), cosine, sine)
    query = query.astype(jnp.bfloat16).reshape(group_rows, query_cols)
    pieces = jnp.stack(
        [projected[:, query_cols : query_cols + part_cols], projected[:, query_cols + part_cols :]]
    )
    part_index = uly_rank % repeats
    for bit_index in range(repeats.bit_length() - 1):
        partner_piece = from_partner(pieces, "uly", bit_index)
        upper_part = part_index >> bit_index & 1 == 1
        pieces = jnp.where(
            upper_part,
            jnp.concatenate([partner_piece, pieces], axis=-1),
            jnp.concatenate([pieces, partner_piece], axis=-1),
        )
    key = rotate(pieces[0][:, None, :], cosine, sine)[:, 0, :].astype(jnp.bfloat16)
    key_value = jnp.concatenate([key, pieces[1].astype(jnp.bfloat16)], axis=1)
    key_value = lax.all_gather(key_value, "blk", axis=0, tiled=True)
    result = attend(
        block_table[0], blk_rank[None].astype(jnp.int32), query, key_value, heads_here, tiles
    )
    merged = lax.all_to_all(result, "uly", split_axis=0, concat_axis=1, tiled=True)
    return merged[None]


def solution(mesh):
    placed = (
        P("dp", ("blk", "uly"), None),
        P("dp", None, None),
        P(("dp", "blk"), "uly"),
        P(("dp", "blk"), "uly"),
        P(("dp", "blk"), "uly"),
    )
    return jax.shard_map(
        shards, mesh=mesh, in_specs=placed, out_specs=P("dp", ("blk", "uly"), None), check_vma=False
    )
```

```python
import functools

import jax
import jax.numpy as jnp
import numpy as np
from jax import lax
from jax.experimental import pallas as pl
from jax.experimental.pallas import tpu as pltpu
from jax.sharding import PartitionSpec as P

H = 16
KV = 4
HD = 128
MBLK = 512
THETA_BASE = 500000.0
LOG2E = 1.4426950408889634
NT = (((1,), (1,)), ((), ()))
TN = (((0,), (0,)), ((), ()))


def from_partner(array, axis, distance):
    return lax.ppermute(array, axis, [(i, i ^ 1 << distance) for i in range(lax.axis_size(axis))])


def angle_tables(positions):
    half_dim = HD // 2
    exponent = jnp.arange(half_dim, dtype=jnp.float32) * (2.0 / HD)
    frequency = jnp.power(jnp.float32(THETA_BASE), -exponent)
    angles = positions.astype(jnp.float32)[:, None] * frequency[None, :]
    return jnp.cos(angles), jnp.sin(angles)


def turn_table(count):
    exponent = np.arange(HD // 2, dtype=np.float32) * np.float32(2.0 / HD)
    frequency = np.power(np.float32(THETA_BASE), -exponent)
    angles = np.arange(count, dtype=np.float32)[:, None] * frequency[None, :]
    cosine, sine = np.cos(angles), np.sin(angles)
    return np.concatenate([cosine, cosine, -sine, sine], axis=1).astype(np.float32)


def rotate(values, cosine, sine):
    cosine, sine = cosine[:, None, :], sine[:, None, :]
    half_dim = HD // 2
    first, second = values[..., :half_dim], values[..., half_dim:]
    return jnp.concatenate([first * cosine - second * sine, second * cosine + first * sine], axis=-1)


def attend_kernel(heads, tiles, table, rank, q_ref, kv_ref, out_ref, best, total, accum):
    scale = HD**-0.5 * LOG2E

    def visit(q_start, key_block, diagonal):
        k_start = pl.multiple_of(key_block * MBLK, MBLK)
        key = kv_ref[pl.ds(k_start, MBLK), :HD]
        value = kv_ref[pl.ds(k_start, MBLK), HD:]
        for head in range(heads):
            cols = pl.ds(head * MBLK, MBLK)
            query = q_ref[pl.ds(q_start, MBLK), head * HD : (head + 1) * HD]
            scores = lax.dot_general(key, query, NT, preferred_element_type=jnp.float32) * scale
            if diagonal:
                key_at = lax.broadcasted_iota(jnp.int32, (MBLK, MBLK), 0)
                query_at = lax.broadcasted_iota(jnp.int32, (MBLK, MBLK), 1)
                scores = jnp.where(key_at <= query_at, scores, -1e30)
                new_best = jnp.max(scores, axis=0, keepdims=True)
            else:
                old_best = best[:, cols]
                new_best = jnp.maximum(old_best, jnp.max(scores, axis=0, keepdims=True))
            weights = jnp.exp2(scores - new_best)
            sums = jnp.sum(weights, axis=0, keepdims=True)
            mixed = lax.dot_general(
                value, weights.astype(jnp.bfloat16), TN, preferred_element_type=jnp.float32
            )
            best[:, cols] = new_best
            if diagonal:
                total[:, cols] = sums
                accum[:, cols] = mixed
            else:
                rescale = jnp.exp2(old_best - new_best)
                total[:, cols] = total[:, cols] * rescale + sums
                accum[:, cols] = accum[:, cols] * rescale + mixed

    for tile in range(tiles):
        q_start = tile * MBLK
        block = rank[0] * tiles + tile
        visit(q_start, block, True)

        @pl.loop(0, block)
        def _(key_block, q_start=q_start, block=block):
            @pl.when(table[block, key_block] > 0)
            def _():
                visit(q_start, key_block, False)

        for head in range(heads):
            cols = pl.ds(head * MBLK, MBLK)
            final = accum[:, cols] / total[:, cols]
            out_ref[pl.ds(q_start, MBLK), head * HD : (head + 1) * HD] = final.T.astype(jnp.bfloat16)


def attend(table, rank, query, key_value, heads, tiles):
    rows = query.shape[0]
    smem = pl.BlockSpec(memory_space=pltpu.SMEM)
    vmem = pl.BlockSpec(memory_space=pltpu.VMEM)
    return pl.pallas_call(
        functools.partial(attend_kernel, heads, tiles),
        out_shape=jax.ShapeDtypeStruct((rows, heads * HD), jnp.bfloat16),
        in_specs=[smem, smem, vmem, vmem],
        out_specs=vmem,
        scratch_shapes=[
            pltpu.VMEM((1, heads * MBLK), jnp.float32),
            pltpu.VMEM((1, heads * MBLK), jnp.float32),
            pltpu.VMEM((HD, heads * MBLK), jnp.float32),
        ],
        compiler_params=pltpu.CompilerParams(vmem_limit_bytes=48 * 1024 * 1024),
        cost_estimate=pl.CostEstimate(flops=8 * 10**9, bytes_accessed=4 * 10**6, transcendentals=16 * 10**6),
    )(table, rank, query, key_value)


PIECE = 256
MESH = pl.DeviceIdType.MESH
IN_FLIGHT = 4


def fused_kernel(
    dp_n, blk_n, table, hid, wq, wk, wv, angles, out,
    weights, rows_all, turns, acc, kv, q_rows, done, best, total, accum,
    local_sem, w_send, w_recv, h_send, h_recv, kv_send, kv_recv, o_send, o_recv,
):
    y, z, u = lax.axis_index("dp"), lax.axis_index("blk"), lax.axis_index("uly")
    last = blk_n - 1
    chunks = dp_n * blk_n
    pieces = weights.shape[0]
    tokens = hid.shape[0]
    depth = wq.shape[0]
    group = rows_all.shape[1]
    up, down, across = {"blk": z + 1}, {"blk": z - 1}, {"dp": 1 - y}
    core = u + 1 - 2 * (u % 2)
    chip = (u + 2) % 4
    far = (core + 2) % 4
    mine = y * blk_n + z
    scale = HD**-0.5 * LOG2E

    barrier = pltpu.get_barrier_semaphore()

    @pl.when(z < last)
    def _():
        pl.semaphore_signal(barrier, inc=1, device_id=up, device_id_type=MESH)

    @pl.when(z > 0)
    def _():
        pl.semaphore_signal(barrier, inc=1, device_id=down, device_id_type=MESH)

    for where in (across, {"uly": core}, {"uly": chip}, {"uly": far}):
        pl.semaphore_signal(barrier, inc=1, device_id=where, device_id_type=MESH)

    own = [
        pltpu.make_async_copy(wk, weights.at[0, mine, :, pl.ds(0, HD)], local_sem.at[0]),
        pltpu.make_async_copy(wv, weights.at[0, mine, :, pl.ds(HD, HD)], local_sem.at[1]),
    ]
    for p in range(1, pieces):
        own.append(
            pltpu.make_async_copy(
                wq.at[:, pl.ds((p - 1) * PIECE, PIECE)], weights.at[p, mine], local_sem.at[p + 1]
            )
        )
    for c in range(chunks):
        own.append(
            pltpu.make_async_copy(
                hid.at[:, pl.ds(c * depth, depth)],
                rows_all.at[c, pl.ds(u * tokens, tokens)],
                local_sem.at[pieces + 1 + c],
            )
        )
    turn_copy = pltpu.make_async_copy(
        angles.at[pl.ds(pl.multiple_of(z * group, group), group)], turns, local_sem.at[pieces + 1 + chunks]
    )
    for copy in own:
        copy.start()
    turn_copy.start()
    middle = jnp.where((z > 0) & (z < last), 1, 0)
    pl.semaphore_wait(barrier, 5 + middle)

    def weight_copy(p, way, source_z, where, rank):
        return pltpu.make_async_remote_copy(
            src_ref=weights.at[p, rank], dst_ref=weights.at[p, rank],
            send_sem=w_send.at[p, way, source_z], recv_sem=w_recv.at[p, rank],
            device_id=where, device_id_type=MESH,
        )

    def hidden_copy(kind, c, source, where):
        part = rows_all.at[c, pl.ds(source * tokens, tokens)]
        return pltpu.make_async_remote_copy(
            src_ref=part, dst_ref=part, send_sem=h_send.at[kind, c], recv_sem=h_recv.at[kind, c],
            device_id={"uly": where}, device_id_type=MESH,
        )

    own_tile = u // 2

    def tile_rows(half):
        tile = own_tile if half == 0 else 1 - own_tile
        return pl.multiple_of(tile * MBLK, MBLK)

    def kv_copy(source_z, half):
        part = kv.at[source_z, pl.ds(tile_rows(half), MBLK)]
        return pltpu.make_async_remote_copy(
            src_ref=part, dst_ref=part,
            send_sem=kv_send.at[half, source_z], recv_sem=kv_recv.at[half, source_z],
            device_id=up, device_id_type=MESH,
        )

    def own_weights(p, finish=False):
        act = (lambda c: c.wait_send()) if finish else (lambda c: c.start())

        @pl.when(z < last)
        def _():
            act(weight_copy(p, 0, z, up, mine))

        @pl.when(z > 0)
        def _():
            act(weight_copy(p, 1, z, down, mine))

        act(weight_copy(p, 2, z, across, mine))

    def pass_on(p, d, finish=False):
        act = (lambda c: c.wait_send()) if finish else (lambda c: c.start())

        @pl.when(z >= d)
        def _():
            rank = y * blk_n + z - d
            if not finish:
                weight_copy(p, 0, z - d, across, rank).wait_recv()

            @pl.when(z < last)
            def _():
                act(weight_copy(p, 0, z - d, up, rank))

            act(weight_copy(p, 2, z - d, across, rank))

        @pl.when(z + d <= last)
        def _():
            rank = y * blk_n + z + d
            if not finish:
                weight_copy(p, 1, z + d, across, rank).wait_recv()

            @pl.when(z > 0)
            def _():
                act(weight_copy(p, 1, z + d, down, rank))

            act(weight_copy(p, 2, z + d, across, rank))

    def across_arrived(p, d):
        other = (1 - y) * blk_n
        if d == 0:
            weight_copy(p, 2, z, across, other + z).wait_recv()
            return

        @pl.when(z >= d)
        def _():
            weight_copy(p, 2, z - d, across, other + z - d).wait_recv()

        @pl.when(z + d <= last)
        def _():
            weight_copy(p, 2, z + d, across, other + z + d).wait_recv()

    def multiply(c):
        @pl.loop(0, group // PIECE)
        def _(i):
            at = pl.ds(pl.multiple_of(i * PIECE, PIECE), PIECE)
            acc[at, :] += jnp.dot(
                rows_all[c, at, :], weights[pieces - 1, c], preferred_element_type=jnp.float32
            )

    def whole_sum(p, at):
        result = jnp.dot(rows_all[0, at, :], weights[p, 0], preferred_element_type=jnp.float32)
        for c in range(1, chunks):
            result += jnp.dot(rows_all[c, at, :], weights[p, c], preferred_element_type=jnp.float32)
        return result

    def turn(values, at):
        return values * turns[at, :HD] + pltpu.roll(values, HD // 2, 1) * turns[at, HD:]

    def kv_half(half):
        @pl.loop(0, MBLK // PIECE)
        def _(i):
            at = pl.ds(pl.multiple_of(tile_rows(half) + i * PIECE, PIECE), PIECE)
            both = whole_sum(0, at)
            kv[z, at, :HD] = turn(both[:, :HD], at).astype(jnp.bfloat16)
            kv[z, at, HD:] = both[:, HD:].astype(jnp.bfloat16)

        @pl.when(z < last)
        def _():
            kv_copy(z, half).start()

    def keep_query(p, at, values):
        for half in range(PIECE // HD):
            col = (p - 1) * PIECE + half * HD
            turned = turn(values[:, half * HD : (half + 1) * HD], at)
            q_rows[at, col : col + HD] = (turned * scale).astype(jnp.bfloat16)

    def whole_queries(lower, upper):
        @pl.loop(lower, upper)
        def _(i):
            at = pl.ds(pl.multiple_of(i * PIECE, PIECE), PIECE)
            for p in range(1, pieces - 1):
                keep_query(p, at, whole_sum(p, at))

    def query_chunks(d):
        across_arrived(pieces - 1, d)
        if d == 0:
            multiply(mine)
            multiply((1 - y) * blk_n + z)
            return

        @pl.when(z >= d)
        def _():
            multiply(y * blk_n + z - d)
            multiply((1 - y) * blk_n + z - d)

        @pl.when(z + d <= last)
        def _():
            multiply(y * blk_n + z + d)
            multiply((1 - y) * blk_n + z + d)

    def kv_pass(d, half):
        @pl.when(z >= d)
        def _():
            kv_copy(z - d, half).wait_recv()

            @pl.when(z < last)
            def _():
                kv_copy(z - d, half).start()

    def hidden_step(lower, upper):
        for c in range(lower, upper):
            hidden_copy(1, c, chip, chip).wait_recv()
            hidden_copy(2, c, chip, core).start()
            if c + IN_FLIGHT < chunks:
                hidden_copy(1, c + IN_FLIGHT, u, chip).start()

    own[0].wait()
    own[1].wait()
    own_weights(0)
    for c in range(chunks):
        own[pieces + 1 + c].wait()
        if c < IN_FLIGHT:
            hidden_copy(1, c, u, chip).start()
    for c in range(chunks):
        hidden_copy(0, c, u, core).start()
    for p in range(1, pieces):
        own[p + 1].wait()
    acc[...] = jnp.zeros_like(acc)
    turn_copy.wait()

    tiles = group // MBLK
    query_cols = q_rows.shape[1]
    pair_heads = PIECE // HD

    def allowance(q_tile, source_z, k_tile):
        allowed = table[z * tiles + q_tile, source_z * tiles + k_tile]
        return jnp.where(allowed > 0, 0.0, -1e30).astype(jnp.float32)

    def visit(pair, q_tile, source_z, k_tiles, first):
        q_at = pl.ds(pl.multiple_of(q_tile * MBLK, MBLK), MBLK)
        parts = [
            kv.at[source_z, pl.ds(pl.multiple_of(k_tile * MBLK, MBLK), MBLK)] for k_tile in k_tiles
        ]
        biases = [0.0 if first else allowance(q_tile, source_z, k_tile) for k_tile in k_tiles]
        for head in range(pair * pair_heads, (pair + 1) * pair_heads):
            cols = slice(head * MBLK, (head + 1) * MBLK)
            query = q_rows[q_at, head * HD : (head + 1) * HD]
            all_scores = []
            new_best = None if first else best[q_tile, :, cols]
            old_best = new_best
            for part, bias in zip(parts, biases):
                scores = lax.dot_general(part[:, :HD], query, NT, preferred_element_type=jnp.float32)
                if first:
                    key_at = lax.broadcasted_iota(jnp.int32, (MBLK, MBLK), 0)
                    query_at = lax.broadcasted_iota(jnp.int32, (MBLK, MBLK), 1)
                    scores = jnp.where(key_at <= query_at, scores, -1e30)
                    new_best = jnp.max(scores, axis=0, keepdims=True)
                else:
                    new_best = jnp.maximum(new_best, jnp.max(scores, axis=0, keepdims=True) + bias)
                all_scores.append(scores)
            sums, mixed = 0.0, 0.0
            for part, bias, scores in zip(parts, biases, all_scores):
                grown = jnp.exp2(scores - (new_best - bias))
                sums += jnp.sum(grown, axis=0, keepdims=True)
                mixed += lax.dot_general(
                    part[:, HD:], grown.astype(jnp.bfloat16), TN, preferred_element_type=jnp.float32
                )
            best[q_tile, :, cols] = new_best
            if first:
                total[q_tile, :, cols] = sums
                accum[q_tile, :, cols] = mixed
            else:
                rescale = jnp.exp2(old_best - new_best)
                total[q_tile, :, cols] = total[q_tile, :, cols] * rescale + sums
                accum[q_tile, :, cols] = accum[q_tile, :, cols] * rescale + mixed

    def out_part(source, pair):
        start = pl.multiple_of(source * query_cols + pair * PIECE, PIECE)
        return out.at[:, pl.ds(start, PIECE)]

    def done_part(owner, pair):
        return done.at[pl.ds(owner * tokens, tokens), pl.ds(pair * PIECE, PIECE)]

    def out_copy(owner, pair):
        return pltpu.make_async_remote_copy(
            src_ref=done_part(owner, pair), dst_ref=out_part(u, pair),
            send_sem=o_send.at[pair, owner], recv_sem=o_recv.at[pair, u],
            device_id={"uly": owner}, device_id_type=MESH,
        )

    def out_arrival(source, pair):
        return pltpu.make_async_remote_copy(
            src_ref=done_part(source, pair), dst_ref=out_part(source, pair),
            send_sem=o_send.at[pair, source], recv_sem=o_recv.at[pair, source],
            device_id={"uly": source}, device_id_type=MESH,
        )

    def out_own(pair):
        return pltpu.make_async_copy(done_part(u, pair), out_part(u, pair), local_sem.at[pair])

    def finalize(pair, q_tile):
        q_at = pl.ds(pl.multiple_of(q_tile * MBLK, MBLK), MBLK)
        for head in range(pair * pair_heads, (pair + 1) * pair_heads):
            cols = slice(head * MBLK, (head + 1) * MBLK)
            final = accum[q_tile, :, cols] / total[q_tile, :, cols]
            done[q_at, head * HD : (head + 1) * HD] = final.T.astype(jnp.bfloat16)
        owners = MBLK // tokens
        for e in range(owners):
            owner = q_tile * owners + e

            @pl.when(owner != u)
            def _():
                out_copy(owner, pair).start()

            @pl.when(owner == u)
            def _():
                out_own(pair).start()

    def attend_own(pair):
        @pl.loop(0, tiles)
        def _(q_tile):
            visit(pair, q_tile, z, [q_tile], True)

            @pl.loop(0, q_tile)
            def _(k_tile):
                visit(pair, q_tile, z, [k_tile], False)

            @pl.when(z == 0)
            def _():
                finalize(pair, q_tile)

    def attend_lower(pair, d):
        @pl.when(z >= d)
        def _():
            @pl.loop(0, tiles)
            def _(q_tile):
                visit(pair, q_tile, z - d, list(range(tiles)), False)

                @pl.when(z == d)
                def _():
                    finalize(pair, q_tile)

    slabs = group // PIECE
    ends = (0, 1, 3, 5, 7, 8)
    step = 0
    for p in range(pieces):
        for d in range(1, blk_n):
            if d == 1 and p + 1 < pieces:
                own_weights(p + 1)
            pass_on(p, d)
            if 0 < step < len(ends):
                hidden_step(ends[step - 1], ends[step])
            if step == 3:
                for e in range(blk_n):
                    across_arrived(0, e)
                for c in range(chunks):
                    hidden_copy(0, c, core, core).wait_recv()
                kv_half(0)
            elif step == 5:
                kv_pass(1, 0)
                for c in range(chunks):
                    hidden_copy(2, c, far, core).wait_recv()
                kv_half(1)
            elif step == 6:
                query_chunks(0)
            elif step == 7:
                kv_pass(2, 0)
                kv_pass(1, 1)
                for e in range(blk_n):
                    across_arrived(1, e)
                whole_queries(0, slabs)
                query_chunks(1)
            elif step == 8:
                attend_own(0)
                query_chunks(2)
                kv_pass(2, 1)
                attend_lower(0, 1)
                query_chunks(3)
            step += 1

    @pl.loop(0, slabs)
    def _(i):
        at = pl.ds(pl.multiple_of(i * PIECE, PIECE), PIECE)
        keep_query(pieces - 1, at, acc[at, :])

    attend_lower(0, 2)
    attend_own(1)
    attend_lower(1, 1)
    kv_pass(3, 0)
    kv_pass(3, 1)
    attend_lower(0, 3)
    attend_lower(1, 2)
    attend_lower(1, 3)

    for p in range(pieces):
        own_weights(p, finish=True)
        for d in range(1, blk_n):
            pass_on(p, d, finish=True)
    for c in range(chunks):
        hidden_copy(0, c, u, core).wait_send()
        hidden_copy(1, c, u, chip).wait_send()
        hidden_copy(2, c, chip, core).wait_send()
    for e in range(blk_n):
        @pl.when(e <= z)
        def _(e=e):
            @pl.when(z < last)
            def _():
                kv_copy(e, 0).wait_send()
                kv_copy(e, 1).wait_send()

    for pair in range(pieces - 1):
        out_own(pair).wait()
        for other in (core, chip, far):
            out_copy(other, pair).wait_send()
            out_arrival(other, pair).wait_recv()


def fused(table, hid, wq, wk, wv, angles, dp_n, blk_n, uly_n):
    tokens, width = hid.shape
    depth, query_cols = wq.shape
    chunks = dp_n * blk_n
    group = tokens * uly_n
    pieces = 1 + query_cols // PIECE
    tiles, heads = group // MBLK, query_cols // HD
    hbm = pl.BlockSpec(memory_space=pl.ANY)
    return pl.pallas_call(
        functools.partial(fused_kernel, dp_n, blk_n),
        out_shape=jax.ShapeDtypeStruct((tokens, uly_n * query_cols), jnp.bfloat16),
        in_specs=[pl.BlockSpec(memory_space=pltpu.SMEM), hbm, hbm, hbm, hbm, hbm],
        out_specs=hbm,
        scratch_shapes=[
            pltpu.VMEM((pieces, chunks, depth, PIECE), jnp.bfloat16),
            pltpu.VMEM((chunks, group, depth), jnp.bfloat16),
            pltpu.VMEM((group, 2 * HD), jnp.float32),
            pltpu.VMEM((group, PIECE), jnp.float32),
            pltpu.VMEM((blk_n, group, 2 * HD), jnp.bfloat16),
            pltpu.VMEM((group, query_cols), jnp.bfloat16),
            pltpu.VMEM((group, query_cols), jnp.bfloat16),
            pltpu.VMEM((tiles, 1, heads * MBLK), jnp.float32),
            pltpu.VMEM((tiles, 1, heads * MBLK), jnp.float32),
            pltpu.VMEM((tiles, HD, heads * MBLK), jnp.float32),
            pltpu.SemaphoreType.DMA((pieces + 2 + chunks,)),
            pltpu.SemaphoreType.DMA((pieces, 3, blk_n)),
            pltpu.SemaphoreType.DMA((pieces, chunks)),
            pltpu.SemaphoreType.DMA((3, chunks)),
            pltpu.SemaphoreType.DMA((3, chunks)),
            pltpu.SemaphoreType.DMA((2, blk_n)),
            pltpu.SemaphoreType.DMA((2, blk_n)),
            pltpu.SemaphoreType.DMA((pieces - 1, uly_n)),
            pltpu.SemaphoreType.DMA((pieces - 1, uly_n)),
        ],
        compiler_params=pltpu.CompilerParams(
            collective_id=0, has_side_effects=True, vmem_limit_bytes=50 * 1024 * 1024
        ),
        cost_estimate=pl.CostEstimate(
            flops=2 * group * width * (query_cols + 2 * HD), bytes_accessed=8 * 10**6, transcendentals=0
        ),
    )(table, hid, wq, wk, wv, angles)


def shards(hidden_states, block_table, w_query, w_key, w_value):
    tokens = hidden_states.shape[1]
    uly_size = lax.axis_size("uly")
    uly_rank = lax.axis_index("uly")
    blk_rank = lax.axis_index("blk")
    heads_here = H // uly_size
    repeats = uly_size // KV
    part_cols = HD // repeats
    query_cols = heads_here * HD
    group_rows = tokens * uly_size
    tiles = group_rows // MBLK
    dp_n, blk_n = lax.axis_size("dp"), lax.axis_size("blk")
    if dp_n == 2 and blk_n == 4 and uly_size == 4 and repeats == 1 and query_cols == 2 * PIECE and tokens * 2 == MBLK:
        merged = fused(
            block_table[0],
            hidden_states[0],
            w_query,
            w_key,
            w_value,
            jnp.asarray(turn_table(blk_n * group_rows)),
            dp_n,
            blk_n,
            uly_size,
        )
        return merged[None]
    w_joined = jnp.concatenate([w_query, w_key, w_value], axis=1)
    w_rows = lax.all_gather(w_joined, ("dp", "blk"), axis=0, tiled=True)
    projected = jnp.dot(
        lax.all_gather(hidden_states[0], "uly", axis=0, tiled=True),
        w_rows,
        preferred_element_type=jnp.float32,
    )
    positions = blk_rank * group_rows + jnp.arange(group_rows, dtype=jnp.int32)
    cosine, sine = angle_tables(positions)
    query = rotate(projected[:, :query_cols].reshape(group_rows, heads_here, HD), cosine, sine)
    query = query.astype(jnp.bfloat16).reshape(group_rows, query_cols)
    pieces = jnp.stack(
        [projected[:, query_cols : query_cols + part_cols], projected[:, query_cols + part_cols :]]
    )
    part_index = uly_rank % repeats
    for bit_index in range(repeats.bit_length() - 1):
        partner_piece = from_partner(pieces, "uly", bit_index)
        upper_part = part_index >> bit_index & 1 == 1
        pieces = jnp.where(
            upper_part,
            jnp.concatenate([partner_piece, pieces], axis=-1),
            jnp.concatenate([pieces, partner_piece], axis=-1),
        )
    key = rotate(pieces[0][:, None, :], cosine, sine)[:, 0, :].astype(jnp.bfloat16)
    key_value = jnp.concatenate([key, pieces[1].astype(jnp.bfloat16)], axis=1)
    key_value = lax.all_gather(key_value, "blk", axis=0, tiled=True)
    result = attend(
        block_table[0], blk_rank[None].astype(jnp.int32), query, key_value, heads_here, tiles
    )
    merged = lax.all_to_all(result, "uly", split_axis=0, concat_axis=1, tiled=True)
    return merged[None]


def solution(mesh):
    placed = (
        P("dp", ("blk", "uly"), None),
        P("dp", None, None),
        P(("dp", "blk"), "uly"),
        P(("dp", "blk"), "uly"),
        P(("dp", "blk"), "uly"),
    )
    return jax.shard_map(
        shards, mesh=mesh, in_specs=placed, out_specs=P("dp", ("blk", "uly"), None), check_vma=False
    )
```

```python
import functools

import jax
import jax.numpy as jnp
import numpy as np
from jax import lax
from jax.experimental import pallas as pl
from jax.experimental.pallas import tpu as pltpu
from jax.sharding import PartitionSpec as P

H = 16
KV = 4
HD = 128
MBLK = 512
THETA_BASE = 500000.0
LOG2E = 1.4426950408889634
NT = (((1,), (1,)), ((), ()))
TN = (((0,), (0,)), ((), ()))


def from_partner(array, axis, distance):
    return lax.ppermute(array, axis, [(i, i ^ 1 << distance) for i in range(lax.axis_size(axis))])


def angle_tables(positions):
    half_dim = HD // 2
    exponent = jnp.arange(half_dim, dtype=jnp.float32) * (2.0 / HD)
    frequency = jnp.power(jnp.float32(THETA_BASE), -exponent)
    angles = positions.astype(jnp.float32)[:, None] * frequency[None, :]
    return jnp.cos(angles), jnp.sin(angles)


def turn_table(count):
    exponent = np.arange(HD // 2, dtype=np.float32) * np.float32(2.0 / HD)
    frequency = np.power(np.float32(THETA_BASE), -exponent)
    angles = np.arange(count, dtype=np.float32)[:, None] * frequency[None, :]
    cosine, sine = np.cos(angles), np.sin(angles)
    return np.concatenate([cosine, cosine, -sine, sine], axis=1).astype(np.float32)


def rotate(values, cosine, sine):
    cosine, sine = cosine[:, None, :], sine[:, None, :]
    half_dim = HD // 2
    first, second = values[..., :half_dim], values[..., half_dim:]
    return jnp.concatenate([first * cosine - second * sine, second * cosine + first * sine], axis=-1)


def attend_kernel(heads, tiles, table, rank, q_ref, kv_ref, out_ref, best, total, accum):
    scale = HD**-0.5 * LOG2E

    def visit(q_start, key_block, diagonal):
        k_start = pl.multiple_of(key_block * MBLK, MBLK)
        key = kv_ref[pl.ds(k_start, MBLK), :HD]
        value = kv_ref[pl.ds(k_start, MBLK), HD:]
        for head in range(heads):
            cols = pl.ds(head * MBLK, MBLK)
            query = q_ref[pl.ds(q_start, MBLK), head * HD : (head + 1) * HD]
            scores = lax.dot_general(key, query, NT, preferred_element_type=jnp.float32) * scale
            if diagonal:
                key_at = lax.broadcasted_iota(jnp.int32, (MBLK, MBLK), 0)
                query_at = lax.broadcasted_iota(jnp.int32, (MBLK, MBLK), 1)
                scores = jnp.where(key_at <= query_at, scores, -1e30)
                new_best = jnp.max(scores, axis=0, keepdims=True)
            else:
                old_best = best[:, cols]
                new_best = jnp.maximum(old_best, jnp.max(scores, axis=0, keepdims=True))
            weights = jnp.exp2(scores - new_best)
            sums = jnp.sum(weights, axis=0, keepdims=True)
            mixed = lax.dot_general(
                value, weights.astype(jnp.bfloat16), TN, preferred_element_type=jnp.float32
            )
            best[:, cols] = new_best
            if diagonal:
                total[:, cols] = sums
                accum[:, cols] = mixed
            else:
                rescale = jnp.exp2(old_best - new_best)
                total[:, cols] = total[:, cols] * rescale + sums
                accum[:, cols] = accum[:, cols] * rescale + mixed

    for tile in range(tiles):
        q_start = tile * MBLK
        block = rank[0] * tiles + tile
        visit(q_start, block, True)

        @pl.loop(0, block)
        def _(key_block, q_start=q_start, block=block):
            @pl.when(table[block, key_block] > 0)
            def _():
                visit(q_start, key_block, False)

        for head in range(heads):
            cols = pl.ds(head * MBLK, MBLK)
            final = accum[:, cols] / total[:, cols]
            out_ref[pl.ds(q_start, MBLK), head * HD : (head + 1) * HD] = final.T.astype(jnp.bfloat16)


def attend(table, rank, query, key_value, heads, tiles):
    rows = query.shape[0]
    smem = pl.BlockSpec(memory_space=pltpu.SMEM)
    vmem = pl.BlockSpec(memory_space=pltpu.VMEM)
    return pl.pallas_call(
        functools.partial(attend_kernel, heads, tiles),
        out_shape=jax.ShapeDtypeStruct((rows, heads * HD), jnp.bfloat16),
        in_specs=[smem, smem, vmem, vmem],
        out_specs=vmem,
        scratch_shapes=[
            pltpu.VMEM((1, heads * MBLK), jnp.float32),
            pltpu.VMEM((1, heads * MBLK), jnp.float32),
            pltpu.VMEM((HD, heads * MBLK), jnp.float32),
        ],
        compiler_params=pltpu.CompilerParams(vmem_limit_bytes=48 * 1024 * 1024),
        cost_estimate=pl.CostEstimate(flops=8 * 10**9, bytes_accessed=4 * 10**6, transcendentals=16 * 10**6),
    )(table, rank, query, key_value)


PIECE = 256
MESH = pl.DeviceIdType.MESH
IN_FLIGHT = 4


def fused_kernel(
    dp_n, blk_n, table, hid, wq, wk, wv, angles, out,
    weights, rows_all, turns, acc, kv, q_rows, done, best, total, accum,
    local_sem, w_send, w_recv, h_send, h_recv, kv_send, kv_recv, o_send, o_recv,
):
    y, z, u = lax.axis_index("dp"), lax.axis_index("blk"), lax.axis_index("uly")
    last = blk_n - 1
    chunks = dp_n * blk_n
    pieces = weights.shape[0]
    tokens = hid.shape[0]
    depth = wq.shape[0]
    group = rows_all.shape[1]
    up, down, across = {"blk": z + 1}, {"blk": z - 1}, {"dp": 1 - y}
    core = u + 1 - 2 * (u % 2)
    chip = (u + 2) % 4
    far = (core + 2) % 4
    mine = y * blk_n + z
    scale = HD**-0.5 * LOG2E

    barrier = pltpu.get_barrier_semaphore()

    for k in range(1, blk_n):
        pl.semaphore_signal(
            barrier, inc=1, device_id={"blk": lax.rem(z + k, blk_n)}, device_id_type=MESH
        )
    for where in (across, {"uly": core}, {"uly": chip}, {"uly": far}):
        pl.semaphore_signal(barrier, inc=1, device_id=where, device_id_type=MESH)

    own = [
        pltpu.make_async_copy(wk, weights.at[0, mine, :, pl.ds(0, HD)], local_sem.at[0]),
        pltpu.make_async_copy(wv, weights.at[0, mine, :, pl.ds(HD, HD)], local_sem.at[1]),
    ]
    for p in range(1, pieces):
        own.append(
            pltpu.make_async_copy(
                wq.at[:, pl.ds((p - 1) * PIECE, PIECE)], weights.at[p, mine], local_sem.at[p + 1]
            )
        )
    for c in range(chunks):
        own.append(
            pltpu.make_async_copy(
                hid.at[:, pl.ds(c * depth, depth)],
                rows_all.at[c, pl.ds(u * tokens, tokens)],
                local_sem.at[pieces + 1 + c],
            )
        )
    turn_copy = pltpu.make_async_copy(
        angles.at[pl.ds(pl.multiple_of(z * group, group), group)], turns, local_sem.at[pieces + 1 + chunks]
    )
    for copy in own:
        copy.start()
    turn_copy.start()
    pl.semaphore_wait(barrier, blk_n + 3)

    def weight_copy(p, way, source_z, where, rank):
        return pltpu.make_async_remote_copy(
            src_ref=weights.at[p, rank], dst_ref=weights.at[p, rank],
            send_sem=w_send.at[p, way, source_z], recv_sem=w_recv.at[p, rank],
            device_id=where, device_id_type=MESH,
        )

    def hidden_copy(kind, c, source, where):
        part = rows_all.at[c, pl.ds(source * tokens, tokens)]
        return pltpu.make_async_remote_copy(
            src_ref=part, dst_ref=part, send_sem=h_send.at[kind, c], recv_sem=h_recv.at[kind, c],
            device_id={"uly": where}, device_id_type=MESH,
        )

    own_tile = u // 2

    def tile_rows(half):
        tile = own_tile if half == 0 else 1 - own_tile
        return pl.multiple_of(tile * MBLK, MBLK)

    def kv_copy(source_z, half, target):
        part = kv.at[source_z, pl.ds(tile_rows(half), MBLK)]
        return pltpu.make_async_remote_copy(
            src_ref=part, dst_ref=part,
            send_sem=kv_send.at[half, target], recv_sem=kv_recv.at[half, source_z],
            device_id={"blk": target}, device_id_type=MESH,
        )

    def own_weights(p, finish=False):
        act = (lambda c: c.wait_send()) if finish else (lambda c: c.start())

        @pl.when(z < last)
        def _():
            act(weight_copy(p, 0, z, up, mine))

        @pl.when(z > 0)
        def _():
            act(weight_copy(p, 1, z, down, mine))

        act(weight_copy(p, 2, z, across, mine))

    def pass_on(p, d, finish=False):
        act = (lambda c: c.wait_send()) if finish else (lambda c: c.start())

        @pl.when(z >= d)
        def _():
            rank = y * blk_n + z - d
            if not finish:
                weight_copy(p, 0, z - d, across, rank).wait_recv()

            @pl.when(z < last)
            def _():
                act(weight_copy(p, 0, z - d, up, rank))

            act(weight_copy(p, 2, z - d, across, rank))

        @pl.when(z + d <= last)
        def _():
            rank = y * blk_n + z + d
            if not finish:
                weight_copy(p, 1, z + d, across, rank).wait_recv()

            @pl.when(z > 0)
            def _():
                act(weight_copy(p, 1, z + d, down, rank))

            act(weight_copy(p, 2, z + d, across, rank))

    def across_arrived(p, d):
        other = (1 - y) * blk_n
        if d == 0:
            weight_copy(p, 2, z, across, other + z).wait_recv()
            return

        @pl.when(z >= d)
        def _():
            weight_copy(p, 2, z - d, across, other + z - d).wait_recv()

        @pl.when(z + d <= last)
        def _():
            weight_copy(p, 2, z + d, across, other + z + d).wait_recv()

    def multiply(c):
        @pl.loop(0, group // PIECE)
        def _(i):
            at = pl.ds(pl.multiple_of(i * PIECE, PIECE), PIECE)
            acc[at, :] += jnp.dot(
                rows_all[c, at, :], weights[pieces - 1, c], preferred_element_type=jnp.float32
            )

    def whole_sum(p, at):
        result = jnp.dot(rows_all[0, at, :], weights[p, 0], preferred_element_type=jnp.float32)
        for c in range(1, chunks):
            result += jnp.dot(rows_all[c, at, :], weights[p, c], preferred_element_type=jnp.float32)
        return result

    def turn(values, at):
        return values * turns[at, :HD] + pltpu.roll(values, HD // 2, 1) * turns[at, HD:]

    def kv_half(half):
        @pl.loop(0, MBLK // PIECE)
        def _(i):
            at = pl.ds(pl.multiple_of(tile_rows(half) + i * PIECE, PIECE), PIECE)
            both = whole_sum(0, at)
            kv[z, at, :HD] = turn(both[:, :HD], at).astype(jnp.bfloat16)
            kv[z, at, HD:] = both[:, HD:].astype(jnp.bfloat16)

        for t in range(1, blk_n):
            @pl.when(z + t <= last)
            def _(t=t):
                kv_copy(z, half, z + t).start()

    def keep_query(p, at, values):
        for half in range(PIECE // HD):
            col = (p - 1) * PIECE + half * HD
            turned = turn(values[:, half * HD : (half + 1) * HD], at)
            q_rows[at, col : col + HD] = (turned * scale).astype(jnp.bfloat16)

    def whole_queries(lower, upper):
        @pl.loop(lower, upper)
        def _(i):
            at = pl.ds(pl.multiple_of(i * PIECE, PIECE), PIECE)
            for p in range(1, pieces - 1):
                keep_query(p, at, whole_sum(p, at))

    def query_chunks(d):
        across_arrived(pieces - 1, d)
        if d == 0:
            multiply(mine)
            multiply((1 - y) * blk_n + z)
            return

        @pl.when(z >= d)
        def _():
            multiply(y * blk_n + z - d)
            multiply((1 - y) * blk_n + z - d)

        @pl.when(z + d <= last)
        def _():
            multiply(y * blk_n + z + d)
            multiply((1 - y) * blk_n + z + d)

    def kv_arrived(d):
        @pl.when(z >= d)
        def _():
            for half in range(2):
                kv_copy(z - d, half, z - d).wait_recv()

    def hidden_step(lower, upper):
        for c in range(lower, upper):
            hidden_copy(1, c, chip, chip).wait_recv()
            hidden_copy(2, c, chip, core).start()
            if c + IN_FLIGHT < chunks:
                hidden_copy(1, c + IN_FLIGHT, u, chip).start()

    own[0].wait()
    own[1].wait()
    own_weights(0)
    for c in range(chunks):
        own[pieces + 1 + c].wait()
        if c < IN_FLIGHT:
            hidden_copy(1, c, u, chip).start()
    for c in range(chunks):
        hidden_copy(0, c, u, core).start()
    for p in range(1, pieces):
        own[p + 1].wait()
    acc[...] = jnp.zeros_like(acc)
    turn_copy.wait()

    tiles = group // MBLK
    query_cols = q_rows.shape[1]
    pair_heads = PIECE // HD

    def allowance(q_tile, source_z, k_tile):
        allowed = table[z * tiles + q_tile, source_z * tiles + k_tile]
        return jnp.where(allowed > 0, 0.0, -1e30).astype(jnp.float32)

    def visit(pair, q_tile, source_z, k_tiles, first):
        q_at = pl.ds(pl.multiple_of(q_tile * MBLK, MBLK), MBLK)
        parts = [
            kv.at[source_z, pl.ds(pl.multiple_of(k_tile * MBLK, MBLK), MBLK)] for k_tile in k_tiles
        ]
        biases = [0.0 if first else allowance(q_tile, source_z, k_tile) for k_tile in k_tiles]
        for head in range(pair * pair_heads, (pair + 1) * pair_heads):
            cols = slice(head * MBLK, (head + 1) * MBLK)
            query = q_rows[q_at, head * HD : (head + 1) * HD]
            all_scores = []
            new_best = None if first else best[q_tile, :, cols]
            old_best = new_best
            for part, bias in zip(parts, biases):
                scores = lax.dot_general(part[:, :HD], query, NT, preferred_element_type=jnp.float32)
                if first:
                    key_at = lax.broadcasted_iota(jnp.int32, (MBLK, MBLK), 0)
                    query_at = lax.broadcasted_iota(jnp.int32, (MBLK, MBLK), 1)
                    scores = jnp.where(key_at <= query_at, scores, -1e30)
                    new_best = jnp.max(scores, axis=0, keepdims=True)
                else:
                    new_best = jnp.maximum(new_best, jnp.max(scores, axis=0, keepdims=True) + bias)
                all_scores.append(scores)
            sums, mixed = 0.0, 0.0
            for part, bias, scores in zip(parts, biases, all_scores):
                grown = jnp.exp2(scores - (new_best - bias))
                sums += jnp.sum(grown, axis=0, keepdims=True)
                mixed += lax.dot_general(
                    part[:, HD:], grown.astype(jnp.bfloat16), TN, preferred_element_type=jnp.float32
                )
            best[q_tile, :, cols] = new_best
            if first:
                total[q_tile, :, cols] = sums
                accum[q_tile, :, cols] = mixed
            else:
                rescale = jnp.exp2(old_best - new_best)
                total[q_tile, :, cols] = total[q_tile, :, cols] * rescale + sums
                accum[q_tile, :, cols] = accum[q_tile, :, cols] * rescale + mixed

    def out_part(source, pair):
        start = pl.multiple_of(source * query_cols + pair * PIECE, PIECE)
        return out.at[:, pl.ds(start, PIECE)]

    def done_part(owner, pair):
        return done.at[pl.ds(owner * tokens, tokens), pl.ds(pair * PIECE, PIECE)]

    def out_copy(owner, pair):
        return pltpu.make_async_remote_copy(
            src_ref=done_part(owner, pair), dst_ref=out_part(u, pair),
            send_sem=o_send.at[pair, owner], recv_sem=o_recv.at[pair, u],
            device_id={"uly": owner}, device_id_type=MESH,
        )

    def out_arrival(source, pair):
        return pltpu.make_async_remote_copy(
            src_ref=done_part(source, pair), dst_ref=out_part(source, pair),
            send_sem=o_send.at[pair, source], recv_sem=o_recv.at[pair, source],
            device_id={"uly": source}, device_id_type=MESH,
        )

    def out_own(pair):
        return pltpu.make_async_copy(done_part(u, pair), out_part(u, pair), local_sem.at[pair])

    def finalize(pair, q_tile):
        q_at = pl.ds(pl.multiple_of(q_tile * MBLK, MBLK), MBLK)
        for head in range(pair * pair_heads, (pair + 1) * pair_heads):
            cols = slice(head * MBLK, (head + 1) * MBLK)
            final = accum[q_tile, :, cols] / total[q_tile, :, cols]
            done[q_at, head * HD : (head + 1) * HD] = final.T.astype(jnp.bfloat16)
        owners = MBLK // tokens
        for e in range(owners):
            owner = q_tile * owners + e

            @pl.when(owner != u)
            def _():
                out_copy(owner, pair).start()

            @pl.when(owner == u)
            def _():
                out_own(pair).start()

    def attend_own(pair):
        @pl.loop(0, tiles)
        def _(q_tile):
            visit(pair, q_tile, z, [q_tile], True)

            @pl.loop(0, q_tile)
            def _(k_tile):
                visit(pair, q_tile, z, [k_tile], False)

            @pl.when(z == 0)
            def _():
                finalize(pair, q_tile)

    def attend_lower(pair, d):
        @pl.when(z >= d)
        def _():
            @pl.loop(0, tiles)
            def _(q_tile):
                visit(pair, q_tile, z - d, list(range(tiles)), False)

                @pl.when(z == d)
                def _():
                    finalize(pair, q_tile)

    slabs = group // PIECE
    ends = (0, 1, 3, 5, 7, 8)
    step = 0
    for p in range(pieces):
        for d in range(1, blk_n):
            if d == 1 and p + 1 < pieces:
                own_weights(p + 1)
            pass_on(p, d)
            if 0 < step < len(ends):
                hidden_step(ends[step - 1], ends[step])
            if step == 3:
                for e in range(blk_n):
                    across_arrived(0, e)
                for c in range(chunks):
                    hidden_copy(0, c, core, core).wait_recv()
                kv_half(0)
            elif step == 5:
                for c in range(chunks):
                    hidden_copy(2, c, far, core).wait_recv()
                kv_half(1)
            elif step == 6:
                query_chunks(0)
            elif step == 7:
                for e in range(blk_n):
                    across_arrived(1, e)
                whole_queries(0, slabs)
                query_chunks(1)
            elif step == 8:
                attend_own(0)
                query_chunks(2)
                kv_arrived(1)
                attend_lower(0, 1)
                query_chunks(3)
            step += 1

    @pl.loop(0, slabs)
    def _(i):
        at = pl.ds(pl.multiple_of(i * PIECE, PIECE), PIECE)
        keep_query(pieces - 1, at, acc[at, :])

    kv_arrived(2)
    attend_lower(0, 2)
    attend_own(1)
    attend_lower(1, 1)
    kv_arrived(3)
    attend_lower(0, 3)
    attend_lower(1, 2)
    attend_lower(1, 3)

    for p in range(pieces):
        own_weights(p, finish=True)
        for d in range(1, blk_n):
            pass_on(p, d, finish=True)
    for c in range(chunks):
        hidden_copy(0, c, u, core).wait_send()
        hidden_copy(1, c, u, chip).wait_send()
        hidden_copy(2, c, chip, core).wait_send()
    for t in range(1, blk_n):
        @pl.when(z + t <= last)
        def _(t=t):
            for half in range(2):
                kv_copy(z, half, z + t).wait_send()

    for pair in range(pieces - 1):
        out_own(pair).wait()
        for other in (core, chip, far):
            out_copy(other, pair).wait_send()
            out_arrival(other, pair).wait_recv()


def fused(table, hid, wq, wk, wv, angles, dp_n, blk_n, uly_n):
    tokens, width = hid.shape
    depth, query_cols = wq.shape
    chunks = dp_n * blk_n
    group = tokens * uly_n
    pieces = 1 + query_cols // PIECE
    tiles, heads = group // MBLK, query_cols // HD
    hbm = pl.BlockSpec(memory_space=pl.ANY)
    return pl.pallas_call(
        functools.partial(fused_kernel, dp_n, blk_n),
        out_shape=jax.ShapeDtypeStruct((tokens, uly_n * query_cols), jnp.bfloat16),
        in_specs=[pl.BlockSpec(memory_space=pltpu.SMEM), hbm, hbm, hbm, hbm, hbm],
        out_specs=hbm,
        scratch_shapes=[
            pltpu.VMEM((pieces, chunks, depth, PIECE), jnp.bfloat16),
            pltpu.VMEM((chunks, group, depth), jnp.bfloat16),
            pltpu.VMEM((group, 2 * HD), jnp.float32),
            pltpu.VMEM((group, PIECE), jnp.float32),
            pltpu.VMEM((blk_n, group, 2 * HD), jnp.bfloat16),
            pltpu.VMEM((group, query_cols), jnp.bfloat16),
            pltpu.VMEM((group, query_cols), jnp.bfloat16),
            pltpu.VMEM((tiles, 1, heads * MBLK), jnp.float32),
            pltpu.VMEM((tiles, 1, heads * MBLK), jnp.float32),
            pltpu.VMEM((tiles, HD, heads * MBLK), jnp.float32),
            pltpu.SemaphoreType.DMA((pieces + 2 + chunks,)),
            pltpu.SemaphoreType.DMA((pieces, 3, blk_n)),
            pltpu.SemaphoreType.DMA((pieces, chunks)),
            pltpu.SemaphoreType.DMA((3, chunks)),
            pltpu.SemaphoreType.DMA((3, chunks)),
            pltpu.SemaphoreType.DMA((2, blk_n)),
            pltpu.SemaphoreType.DMA((2, blk_n)),
            pltpu.SemaphoreType.DMA((pieces - 1, uly_n)),
            pltpu.SemaphoreType.DMA((pieces - 1, uly_n)),
        ],
        compiler_params=pltpu.CompilerParams(
            collective_id=0, has_side_effects=True, vmem_limit_bytes=60 * 1024 * 1024
        ),
        cost_estimate=pl.CostEstimate(
            flops=2 * group * width * (query_cols + 2 * HD), bytes_accessed=8 * 10**6, transcendentals=0
        ),
    )(table, hid, wq, wk, wv, angles)


def shards(hidden_states, block_table, w_query, w_key, w_value):
    tokens = hidden_states.shape[1]
    uly_size = lax.axis_size("uly")
    uly_rank = lax.axis_index("uly")
    blk_rank = lax.axis_index("blk")
    heads_here = H // uly_size
    repeats = uly_size // KV
    part_cols = HD // repeats
    query_cols = heads_here * HD
    group_rows = tokens * uly_size
    tiles = group_rows // MBLK
    dp_n, blk_n = lax.axis_size("dp"), lax.axis_size("blk")
    if dp_n == 2 and blk_n == 4 and uly_size == 4 and repeats == 1 and query_cols == 2 * PIECE and tokens * 2 == MBLK:
        merged = fused(
            block_table[0],
            hidden_states[0],
            w_query,
            w_key,
            w_value,
            jnp.asarray(turn_table(blk_n * group_rows)),
            dp_n,
            blk_n,
            uly_size,
        )
        return merged[None]
    w_joined = jnp.concatenate([w_query, w_key, w_value], axis=1)
    w_rows = lax.all_gather(w_joined, ("dp", "blk"), axis=0, tiled=True)
    projected = jnp.dot(
        lax.all_gather(hidden_states[0], "uly", axis=0, tiled=True),
        w_rows,
        preferred_element_type=jnp.float32,
    )
    positions = blk_rank * group_rows + jnp.arange(group_rows, dtype=jnp.int32)
    cosine, sine = angle_tables(positions)
    query = rotate(projected[:, :query_cols].reshape(group_rows, heads_here, HD), cosine, sine)
    query = query.astype(jnp.bfloat16).reshape(group_rows, query_cols)
    pieces = jnp.stack(
        [projected[:, query_cols : query_cols + part_cols], projected[:, query_cols + part_cols :]]
    )
    part_index = uly_rank % repeats
    for bit_index in range(repeats.bit_length() - 1):
        partner_piece = from_partner(pieces, "uly", bit_index)
        upper_part = part_index >> bit_index & 1 == 1
        pieces = jnp.where(
            upper_part,
            jnp.concatenate([partner_piece, pieces], axis=-1),
            jnp.concatenate([pieces, partner_piece], axis=-1),
        )
    key = rotate(pieces[0][:, None, :], cosine, sine)[:, 0, :].astype(jnp.bfloat16)
    key_value = jnp.concatenate([key, pieces[1].astype(jnp.bfloat16)], axis=1)
    key_value = lax.all_gather(key_value, "blk", axis=0, tiled=True)
    result = attend(
        block_table[0], blk_rank[None].astype(jnp.int32), query, key_value, heads_here, tiles
    )
    merged = lax.all_to_all(result, "uly", split_axis=0, concat_axis=1, tiled=True)
    return merged[None]


def solution(mesh):
    placed = (
        P("dp", ("blk", "uly"), None),
        P("dp", None, None),
        P(("dp", "blk"), "uly"),
        P(("dp", "blk"), "uly"),
        P(("dp", "blk"), "uly"),
    )
    return jax.shard_map(
        shards, mesh=mesh, in_specs=placed, out_specs=P("dp", ("blk", "uly"), None), check_vma=False
    )
```

```python
import functools

import jax
import jax.numpy as jnp
import numpy as np
from jax import lax
from jax.experimental import pallas as pl
from jax.experimental.pallas import tpu as pltpu
from jax.sharding import PartitionSpec as P

H = 16
KV = 4
HD = 128
MBLK = 512
THETA_BASE = 500000.0
LOG2E = 1.4426950408889634
NT = (((1,), (1,)), ((), ()))
TN = (((0,), (0,)), ((), ()))


def from_partner(array, axis, distance):
    return lax.ppermute(array, axis, [(i, i ^ 1 << distance) for i in range(lax.axis_size(axis))])


def angle_tables(positions):
    half_dim = HD // 2
    exponent = jnp.arange(half_dim, dtype=jnp.float32) * (2.0 / HD)
    frequency = jnp.power(jnp.float32(THETA_BASE), -exponent)
    angles = positions.astype(jnp.float32)[:, None] * frequency[None, :]
    return jnp.cos(angles), jnp.sin(angles)


def turn_table(count):
    exponent = np.arange(HD // 2, dtype=np.float32) * np.float32(2.0 / HD)
    frequency = np.power(np.float32(THETA_BASE), -exponent)
    angles = np.arange(count, dtype=np.float32)[:, None] * frequency[None, :]
    cosine, sine = np.cos(angles), np.sin(angles)
    return np.concatenate([cosine, cosine, -sine, sine], axis=1).astype(np.float32)


def rotate(values, cosine, sine):
    cosine, sine = cosine[:, None, :], sine[:, None, :]
    half_dim = HD // 2
    first, second = values[..., :half_dim], values[..., half_dim:]
    return jnp.concatenate([first * cosine - second * sine, second * cosine + first * sine], axis=-1)


def attend_kernel(heads, tiles, table, rank, q_ref, kv_ref, out_ref, best, total, accum):
    scale = HD**-0.5 * LOG2E

    def visit(q_start, key_block, diagonal):
        k_start = pl.multiple_of(key_block * MBLK, MBLK)
        key = kv_ref[pl.ds(k_start, MBLK), :HD]
        value = kv_ref[pl.ds(k_start, MBLK), HD:]
        for head in range(heads):
            cols = pl.ds(head * MBLK, MBLK)
            query = q_ref[pl.ds(q_start, MBLK), head * HD : (head + 1) * HD]
            scores = lax.dot_general(key, query, NT, preferred_element_type=jnp.float32) * scale
            if diagonal:
                key_at = lax.broadcasted_iota(jnp.int32, (MBLK, MBLK), 0)
                query_at = lax.broadcasted_iota(jnp.int32, (MBLK, MBLK), 1)
                scores = jnp.where(key_at <= query_at, scores, -1e30)
                new_best = jnp.max(scores, axis=0, keepdims=True)
            else:
                old_best = best[:, cols]
                new_best = jnp.maximum(old_best, jnp.max(scores, axis=0, keepdims=True))
            weights = jnp.exp2(scores - new_best)
            sums = jnp.sum(weights, axis=0, keepdims=True)
            mixed = lax.dot_general(
                value, weights.astype(jnp.bfloat16), TN, preferred_element_type=jnp.float32
            )
            best[:, cols] = new_best
            if diagonal:
                total[:, cols] = sums
                accum[:, cols] = mixed
            else:
                rescale = jnp.exp2(old_best - new_best)
                total[:, cols] = total[:, cols] * rescale + sums
                accum[:, cols] = accum[:, cols] * rescale + mixed

    for tile in range(tiles):
        q_start = tile * MBLK
        block = rank[0] * tiles + tile
        visit(q_start, block, True)

        @pl.loop(0, block)
        def _(key_block, q_start=q_start, block=block):
            @pl.when(table[block, key_block] > 0)
            def _():
                visit(q_start, key_block, False)

        for head in range(heads):
            cols = pl.ds(head * MBLK, MBLK)
            final = accum[:, cols] / total[:, cols]
            out_ref[pl.ds(q_start, MBLK), head * HD : (head + 1) * HD] = final.T.astype(jnp.bfloat16)


def attend(table, rank, query, key_value, heads, tiles):
    rows = query.shape[0]
    smem = pl.BlockSpec(memory_space=pltpu.SMEM)
    vmem = pl.BlockSpec(memory_space=pltpu.VMEM)
    return pl.pallas_call(
        functools.partial(attend_kernel, heads, tiles),
        out_shape=jax.ShapeDtypeStruct((rows, heads * HD), jnp.bfloat16),
        in_specs=[smem, smem, vmem, vmem],
        out_specs=vmem,
        scratch_shapes=[
            pltpu.VMEM((1, heads * MBLK), jnp.float32),
            pltpu.VMEM((1, heads * MBLK), jnp.float32),
            pltpu.VMEM((HD, heads * MBLK), jnp.float32),
        ],
        compiler_params=pltpu.CompilerParams(vmem_limit_bytes=48 * 1024 * 1024),
        cost_estimate=pl.CostEstimate(flops=8 * 10**9, bytes_accessed=4 * 10**6, transcendentals=16 * 10**6),
    )(table, rank, query, key_value)


PIECE = 256
MESH = pl.DeviceIdType.MESH
IN_FLIGHT = 4


def fused_kernel(
    dp_n, blk_n, table, hid, wq, wk, wv, angles, out,
    weights, rows_all, turns, acc, kv, q_rows, done, best, total, accum,
    local_sem, w_send, w_recv, h_send, h_recv, kv_send, kv_recv, o_send, o_recv,
):
    y, z, u = lax.axis_index("dp"), lax.axis_index("blk"), lax.axis_index("uly")
    last = blk_n - 1
    chunks = dp_n * blk_n
    pieces = weights.shape[0]
    tokens = hid.shape[0]
    depth = wq.shape[0]
    group = rows_all.shape[1]
    up, down, across = {"blk": z + 1}, {"blk": z - 1}, {"dp": 1 - y}
    core = u + 1 - 2 * (u % 2)
    chip = (u + 2) % 4
    far = (core + 2) % 4
    mine = y * blk_n + z
    scale = HD**-0.5 * LOG2E

    barrier = pltpu.get_barrier_semaphore()

    @pl.when(z < last)
    def _():
        pl.semaphore_signal(barrier, inc=1, device_id=up, device_id_type=MESH)

    @pl.when(z > 0)
    def _():
        pl.semaphore_signal(barrier, inc=1, device_id=down, device_id_type=MESH)

    for where in (across, {"uly": core}, {"uly": chip}, {"uly": far}):
        pl.semaphore_signal(barrier, inc=1, device_id=where, device_id_type=MESH)

    own = [
        pltpu.make_async_copy(wk, weights.at[0, mine, :, pl.ds(0, HD)], local_sem.at[0]),
        pltpu.make_async_copy(wv, weights.at[0, mine, :, pl.ds(HD, HD)], local_sem.at[1]),
    ]
    for p in range(1, pieces):
        own.append(
            pltpu.make_async_copy(
                wq.at[:, pl.ds((p - 1) * PIECE, PIECE)], weights.at[p, mine], local_sem.at[p + 1]
            )
        )
    for c in range(chunks):
        own.append(
            pltpu.make_async_copy(
                hid.at[:, pl.ds(c * depth, depth)],
                rows_all.at[c, pl.ds(u * tokens, tokens)],
                local_sem.at[pieces + 1 + c],
            )
        )
    turn_copy = pltpu.make_async_copy(
        angles.at[pl.ds(pl.multiple_of(z * group, group), group)], turns, local_sem.at[pieces + 1 + chunks]
    )
    for copy in own:
        copy.start()
    turn_copy.start()
    middle = jnp.where((z > 0) & (z < last), 1, 0)
    pl.semaphore_wait(barrier, 5 + middle)

    def weight_copy(p, way, source_z, where, rank):
        return pltpu.make_async_remote_copy(
            src_ref=weights.at[p, rank], dst_ref=weights.at[p, rank],
            send_sem=w_send.at[p, way, source_z], recv_sem=w_recv.at[p, rank],
            device_id=where, device_id_type=MESH,
        )

    def hidden_copy(kind, c, source, where):
        part = rows_all.at[c, pl.ds(source * tokens, tokens)]
        return pltpu.make_async_remote_copy(
            src_ref=part, dst_ref=part, send_sem=h_send.at[kind, c], recv_sem=h_recv.at[kind, c],
            device_id={"uly": where}, device_id_type=MESH,
        )

    own_tile = u // 2

    def tile_rows(half):
        tile = own_tile if half == 0 else 1 - own_tile
        return pl.multiple_of(tile * MBLK, MBLK)

    def kv_copy(source_z, half):
        part = kv.at[source_z, pl.ds(tile_rows(half), MBLK)]
        return pltpu.make_async_remote_copy(
            src_ref=part, dst_ref=part,
            send_sem=kv_send.at[half, source_z], recv_sem=kv_recv.at[half, source_z],
            device_id=up, device_id_type=MESH,
        )

    def own_weights(p, finish=False):
        act = (lambda c: c.wait_send()) if finish else (lambda c: c.start())

        @pl.when(z < last)
        def _():
            act(weight_copy(p, 0, z, up, mine))

        @pl.when(z > 0)
        def _():
            act(weight_copy(p, 1, z, down, mine))

        act(weight_copy(p, 2, z, across, mine))

    def pass_on(p, d, finish=False):
        act = (lambda c: c.wait_send()) if finish else (lambda c: c.start())

        @pl.when(z >= d)
        def _():
            rank = y * blk_n + z - d
            if not finish:
                weight_copy(p, 0, z - d, across, rank).wait_recv()

            @pl.when(z < last)
            def _():
                act(weight_copy(p, 0, z - d, up, rank))

            act(weight_copy(p, 2, z - d, across, rank))

        @pl.when(z + d <= last)
        def _():
            rank = y * blk_n + z + d
            if not finish:
                weight_copy(p, 1, z + d, across, rank).wait_recv()

            @pl.when(z > 0)
            def _():
                act(weight_copy(p, 1, z + d, down, rank))

            act(weight_copy(p, 2, z + d, across, rank))

    def across_arrived(p, d):
        other = (1 - y) * blk_n
        if d == 0:
            weight_copy(p, 2, z, across, other + z).wait_recv()
            return

        @pl.when(z >= d)
        def _():
            weight_copy(p, 2, z - d, across, other + z - d).wait_recv()

        @pl.when(z + d <= last)
        def _():
            weight_copy(p, 2, z + d, across, other + z + d).wait_recv()

    def multiply(c):
        @pl.loop(0, group // PIECE)
        def _(i):
            at = pl.ds(pl.multiple_of(i * PIECE, PIECE), PIECE)
            acc[at, :] += jnp.dot(
                rows_all[c, at, :], weights[pieces - 1, c], preferred_element_type=jnp.float32
            )

    def whole_sum(p, at):
        result = jnp.dot(rows_all[0, at, :], weights[p, 0], preferred_element_type=jnp.float32)
        for c in range(1, chunks):
            result += jnp.dot(rows_all[c, at, :], weights[p, c], preferred_element_type=jnp.float32)
        return result

    def turn(values, at):
        return values * turns[at, :HD] + pltpu.roll(values, HD // 2, 1) * turns[at, HD:]

    def kv_half(half):
        @pl.loop(0, MBLK // PIECE)
        def _(i):
            at = pl.ds(pl.multiple_of(tile_rows(half) + i * PIECE, PIECE), PIECE)
            both = whole_sum(0, at)
            kv[z, at, :HD] = turn(both[:, :HD], at).astype(jnp.bfloat16)
            kv[z, at, HD:] = both[:, HD:].astype(jnp.bfloat16)

        @pl.when(z < last)
        def _():
            kv_copy(z, half).start()

    def keep_query(p, at, values):
        for half in range(PIECE // HD):
            col = (p - 1) * PIECE + half * HD
            turned = turn(values[:, half * HD : (half + 1) * HD], at)
            q_rows[at, col : col + HD] = (turned * scale).astype(jnp.bfloat16)

    def whole_queries(lower, upper):
        @pl.loop(lower, upper)
        def _(i):
            at = pl.ds(pl.multiple_of(i * PIECE, PIECE), PIECE)
            for p in range(1, pieces - 1):
                keep_query(p, at, whole_sum(p, at))

    def query_chunks(d):
        across_arrived(pieces - 1, d)
        if d == 0:
            multiply(mine)
            multiply((1 - y) * blk_n + z)
            return

        @pl.when(z >= d)
        def _():
            multiply(y * blk_n + z - d)
            multiply((1 - y) * blk_n + z - d)

        @pl.when(z + d <= last)
        def _():
            multiply(y * blk_n + z + d)
            multiply((1 - y) * blk_n + z + d)

    def kv_pass(d, half):
        @pl.when(z >= d)
        def _():
            kv_copy(z - d, half).wait_recv()

            @pl.when(z < last)
            def _():
                kv_copy(z - d, half).start()

    def hidden_step(lower, upper):
        for c in range(lower, upper):
            hidden_copy(1, c, chip, chip).wait_recv()
            hidden_copy(2, c, chip, core).start()
            if c + IN_FLIGHT < chunks:
                hidden_copy(1, c + IN_FLIGHT, u, chip).start()

    own[0].wait()
    own[1].wait()
    own_weights(0)
    for c in range(chunks):
        own[pieces + 1 + c].wait()
        if c < IN_FLIGHT:
            hidden_copy(1, c, u, chip).start()
    for c in range(chunks):
        hidden_copy(0, c, u, core).start()
    for p in range(1, pieces):
        own[p + 1].wait()
    acc[...] = jnp.zeros_like(acc)
    turn_copy.wait()

    tiles = group // MBLK
    query_cols = q_rows.shape[1]
    pair_heads = PIECE // HD

    def allowance(q_tile, source_z, k_tile):
        allowed = table[z * tiles + q_tile, source_z * tiles + k_tile]
        return jnp.where(allowed > 0, 0.0, -1e30).astype(jnp.float32)

    def visit(pair, q_tile, source_z, k_tiles, first):
        q_at = pl.ds(pl.multiple_of(q_tile * MBLK, MBLK), MBLK)
        parts = [
            kv.at[source_z, pl.ds(pl.multiple_of(k_tile * MBLK, MBLK), MBLK)] for k_tile in k_tiles
        ]
        biases = [0.0 if first else allowance(q_tile, source_z, k_tile) for k_tile in k_tiles]
        for head in range(pair * pair_heads, (pair + 1) * pair_heads):
            cols = slice(head * MBLK, (head + 1) * MBLK)
            query = q_rows[q_at, head * HD : (head + 1) * HD]
            all_scores = []
            new_best = None if first else best[q_tile, :, cols]
            old_best = new_best
            for part, bias in zip(parts, biases):
                scores = lax.dot_general(part[:, :HD], query, NT, preferred_element_type=jnp.float32)
                if first:
                    key_at = lax.broadcasted_iota(jnp.int32, (MBLK, MBLK), 0)
                    query_at = lax.broadcasted_iota(jnp.int32, (MBLK, MBLK), 1)
                    scores = jnp.where(key_at <= query_at, scores, -1e30)
                    new_best = jnp.max(scores, axis=0, keepdims=True)
                else:
                    new_best = jnp.maximum(new_best, jnp.max(scores, axis=0, keepdims=True) + bias)
                all_scores.append(scores)
            sums, mixed = 0.0, 0.0
            for part, bias, scores in zip(parts, biases, all_scores):
                grown = jnp.exp2(scores - (new_best - bias))
                sums += jnp.sum(grown, axis=0, keepdims=True)
                mixed += lax.dot_general(
                    part[:, HD:], grown.astype(jnp.bfloat16), TN, preferred_element_type=jnp.float32
                )
            best[q_tile, :, cols] = new_best
            if first:
                total[q_tile, :, cols] = sums
                accum[q_tile, :, cols] = mixed
            else:
                rescale = jnp.exp2(old_best - new_best)
                total[q_tile, :, cols] = total[q_tile, :, cols] * rescale + sums
                accum[q_tile, :, cols] = accum[q_tile, :, cols] * rescale + mixed

    def out_part(source, pair):
        start = pl.multiple_of(source * query_cols + pair * PIECE, PIECE)
        return out.at[:, pl.ds(start, PIECE)]

    def done_part(owner, pair):
        return done.at[pl.ds(owner * tokens, tokens), pl.ds(pair * PIECE, PIECE)]

    def out_copy(owner, pair):
        return pltpu.make_async_remote_copy(
            src_ref=done_part(owner, pair), dst_ref=out_part(u, pair),
            send_sem=o_send.at[pair, owner], recv_sem=o_recv.at[pair, u],
            device_id={"uly": owner}, device_id_type=MESH,
        )

    def out_arrival(source, pair):
        return pltpu.make_async_remote_copy(
            src_ref=done_part(source, pair), dst_ref=out_part(source, pair),
            send_sem=o_send.at[pair, source], recv_sem=o_recv.at[pair, source],
            device_id={"uly": source}, device_id_type=MESH,
        )

    def out_own(pair):
        return pltpu.make_async_copy(done_part(u, pair), out_part(u, pair), local_sem.at[pair])

    def finalize(pair, q_tile):
        q_at = pl.ds(pl.multiple_of(q_tile * MBLK, MBLK), MBLK)
        for head in range(pair * pair_heads, (pair + 1) * pair_heads):
            cols = slice(head * MBLK, (head + 1) * MBLK)
            final = accum[q_tile, :, cols] / total[q_tile, :, cols]
            done[q_at, head * HD : (head + 1) * HD] = final.T.astype(jnp.bfloat16)
        owners = MBLK // tokens
        for e in range(owners):
            owner = q_tile * owners + e

            @pl.when(owner != u)
            def _():
                out_copy(owner, pair).start()

            @pl.when(owner == u)
            def _():
                out_own(pair).start()

    def attend_own(pair):
        @pl.loop(0, tiles)
        def _(q_tile):
            visit(pair, q_tile, z, [q_tile], True)

            @pl.loop(0, q_tile)
            def _(k_tile):
                visit(pair, q_tile, z, [k_tile], False)

            @pl.when(z == 0)
            def _():
                finalize(pair, q_tile)

    def attend_lower(pair, d):
        @pl.when(z >= d)
        def _():
            @pl.loop(0, tiles)
            def _(q_tile):
                visit(pair, q_tile, z - d, list(range(tiles)), False)

                @pl.when(z == d)
                def _():
                    finalize(pair, q_tile)

    slabs = group // PIECE
    ends = (0, 1, 3, 5, 7, 8)
    step = 0
    for p in range(pieces):
        for d in range(1, blk_n):
            if d == 1 and p + 1 < pieces:
                own_weights(p + 1)
            pass_on(p, d)
            if 0 < step < len(ends):
                hidden_step(ends[step - 1], ends[step])
            if step == 3:
                for e in range(blk_n):
                    across_arrived(0, e)
                for c in range(chunks):
                    hidden_copy(0, c, core, core).wait_recv()
                kv_half(0)
            elif step == 5:
                kv_pass(1, 0)
                for c in range(chunks):
                    hidden_copy(2, c, far, core).wait_recv()
                kv_half(1)
            elif step == 6:
                query_chunks(0)
            elif step == 7:
                kv_pass(2, 0)
                kv_pass(1, 1)
                for e in range(blk_n):
                    across_arrived(1, e)
                whole_queries(0, slabs)
                query_chunks(1)
            elif step == 8:
                attend_own(0)
                kv_pass(2, 1)
                query_chunks(2)
                attend_lower(0, 1)
                query_chunks(3)
            step += 1

    @pl.loop(0, slabs)
    def _(i):
        at = pl.ds(pl.multiple_of(i * PIECE, PIECE), PIECE)
        keep_query(pieces - 1, at, acc[at, :])

    attend_lower(0, 2)
    attend_own(1)
    attend_lower(1, 1)
    kv_pass(3, 0)
    kv_pass(3, 1)
    attend_lower(0, 3)
    attend_lower(1, 2)
    attend_lower(1, 3)

    for p in range(pieces):
        own_weights(p, finish=True)
        for d in range(1, blk_n):
            pass_on(p, d, finish=True)
    for c in range(chunks):
        hidden_copy(0, c, u, core).wait_send()
        hidden_copy(1, c, u, chip).wait_send()
        hidden_copy(2, c, chip, core).wait_send()
    for e in range(blk_n):
        @pl.when(e <= z)
        def _(e=e):
            @pl.when(z < last)
            def _():
                kv_copy(e, 0).wait_send()
                kv_copy(e, 1).wait_send()

    for pair in range(pieces - 1):
        out_own(pair).wait()
        for other in (core, chip, far):
            out_copy(other, pair).wait_send()
            out_arrival(other, pair).wait_recv()


def fused(table, hid, wq, wk, wv, angles, dp_n, blk_n, uly_n):
    tokens, width = hid.shape
    depth, query_cols = wq.shape
    chunks = dp_n * blk_n
    group = tokens * uly_n
    pieces = 1 + query_cols // PIECE
    tiles, heads = group // MBLK, query_cols // HD
    hbm = pl.BlockSpec(memory_space=pl.ANY)
    return pl.pallas_call(
        functools.partial(fused_kernel, dp_n, blk_n),
        out_shape=jax.ShapeDtypeStruct((tokens, uly_n * query_cols), jnp.bfloat16),
        in_specs=[pl.BlockSpec(memory_space=pltpu.SMEM), hbm, hbm, hbm, hbm, hbm],
        out_specs=hbm,
        scratch_shapes=[
            pltpu.VMEM((pieces, chunks, depth, PIECE), jnp.bfloat16),
            pltpu.VMEM((chunks, group, depth), jnp.bfloat16),
            pltpu.VMEM((group, 2 * HD), jnp.float32),
            pltpu.VMEM((group, PIECE), jnp.float32),
            pltpu.VMEM((blk_n, group, 2 * HD), jnp.bfloat16),
            pltpu.VMEM((group, query_cols), jnp.bfloat16),
            pltpu.VMEM((group, query_cols), jnp.bfloat16),
            pltpu.VMEM((tiles, 1, heads * MBLK), jnp.float32),
            pltpu.VMEM((tiles, 1, heads * MBLK), jnp.float32),
            pltpu.VMEM((tiles, HD, heads * MBLK), jnp.float32),
            pltpu.SemaphoreType.DMA((pieces + 2 + chunks,)),
            pltpu.SemaphoreType.DMA((pieces, 3, blk_n)),
            pltpu.SemaphoreType.DMA((pieces, chunks)),
            pltpu.SemaphoreType.DMA((3, chunks)),
            pltpu.SemaphoreType.DMA((3, chunks)),
            pltpu.SemaphoreType.DMA((2, blk_n)),
            pltpu.SemaphoreType.DMA((2, blk_n)),
            pltpu.SemaphoreType.DMA((pieces - 1, uly_n)),
            pltpu.SemaphoreType.DMA((pieces - 1, uly_n)),
        ],
        compiler_params=pltpu.CompilerParams(
            collective_id=0, has_side_effects=True, vmem_limit_bytes=60 * 1024 * 1024
        ),
        cost_estimate=pl.CostEstimate(
            flops=2 * group * width * (query_cols + 2 * HD), bytes_accessed=8 * 10**6, transcendentals=0
        ),
    )(table, hid, wq, wk, wv, angles)


def shards(hidden_states, block_table, w_query, w_key, w_value):
    tokens = hidden_states.shape[1]
    uly_size = lax.axis_size("uly")
    uly_rank = lax.axis_index("uly")
    blk_rank = lax.axis_index("blk")
    heads_here = H // uly_size
    repeats = uly_size // KV
    part_cols = HD // repeats
    query_cols = heads_here * HD
    group_rows = tokens * uly_size
    tiles = group_rows // MBLK
    dp_n, blk_n = lax.axis_size("dp"), lax.axis_size("blk")
    if dp_n == 2 and blk_n == 4 and uly_size == 4 and repeats == 1 and query_cols == 2 * PIECE and tokens * 2 == MBLK:
        merged = fused(
            block_table[0],
            hidden_states[0],
            w_query,
            w_key,
            w_value,
            jnp.asarray(turn_table(blk_n * group_rows)),
            dp_n,
            blk_n,
            uly_size,
        )
        return merged[None]
    w_joined = jnp.concatenate([w_query, w_key, w_value], axis=1)
    w_rows = lax.all_gather(w_joined, ("dp", "blk"), axis=0, tiled=True)
    projected = jnp.dot(
        lax.all_gather(hidden_states[0], "uly", axis=0, tiled=True),
        w_rows,
        preferred_element_type=jnp.float32,
    )
    positions = blk_rank * group_rows + jnp.arange(group_rows, dtype=jnp.int32)
    cosine, sine = angle_tables(positions)
    query = rotate(projected[:, :query_cols].reshape(group_rows, heads_here, HD), cosine, sine)
    query = query.astype(jnp.bfloat16).reshape(group_rows, query_cols)
    pieces = jnp.stack(
        [projected[:, query_cols : query_cols + part_cols], projected[:, query_cols + part_cols :]]
    )
    part_index = uly_rank % repeats
    for bit_index in range(repeats.bit_length() - 1):
        partner_piece = from_partner(pieces, "uly", bit_index)
        upper_part = part_index >> bit_index & 1 == 1
        pieces = jnp.where(
            upper_part,
            jnp.concatenate([partner_piece, pieces], axis=-1),
            jnp.concatenate([pieces, partner_piece], axis=-1),
        )
    key = rotate(pieces[0][:, None, :], cosine, sine)[:, 0, :].astype(jnp.bfloat16)
    key_value = jnp.concatenate([key, pieces[1].astype(jnp.bfloat16)], axis=1)
    key_value = lax.all_gather(key_value, "blk", axis=0, tiled=True)
    result = attend(
        block_table[0], blk_rank[None].astype(jnp.int32), query, key_value, heads_here, tiles
    )
    merged = lax.all_to_all(result, "uly", split_axis=0, concat_axis=1, tiled=True)
    return merged[None]


def solution(mesh):
    placed = (
        P("dp", ("blk", "uly"), None),
        P("dp", None, None),
        P(("dp", "blk"), "uly"),
        P(("dp", "blk"), "uly"),
        P(("dp", "blk"), "uly"),
    )
    return jax.shard_map(
        shards, mesh=mesh, in_specs=placed, out_specs=P("dp", ("blk", "uly"), None), check_vma=False
    )
```
